32 devices in a mesh: parts: 2 (over y), expert: 4 (over x, core), etp: 4 (over z).
Axes of the slice: x: 2, y: 2, z: 4, core: 2. Of those that a mesh axis runs over, the one named last changes fastest.
Arguments:
- out_grad: bfloat16 [512, 3072], P(('parts', 'expert'), 'etp'), parts along dimension 0, may hold values from -6 to 6
- router_logits: float32 [512, 2], P(('parts', 'expert')), parts along dimension 0, may hold values from -6 to 6
- slot_of: int32 [512, 2], P(('parts', 'expert')), parts along dimension 0, may hold values from 0 to 3, all different within a row; in each aligned block of 64 rows (0 to 63, 64 to 127, ...) at most 64 rows name the same one
- gate_pre: bfloat16 [2048, 2048], P(('parts', 'expert'), 'etp'), parts along dimension 0, may hold values from -6 to 6
- up_pre: bfloat16 [2048, 2048], P(('parts', 'expert'), 'etp'), parts along dimension 0, may hold values from -6 to 6
- down_weight: bfloat16 [4, 2048, 3072], P('expert', 'etp'), may hold values from -0.125 to 0.125
Outputs:
- grad_gate: bfloat16 [2048, 2048], P(('parts', 'expert'), 'etp'), parts along dimension 0
- grad_up: bfloat16 [2048, 2048], P(('parts', 'expert'), 'etp'), parts along dimension 0
- logit_grad: float32 [512, 2], P(('parts', 'expert')), parts along dimension 0
The draws below stay inside these ranges and needn't reach their ends.
There are 2 independent parts, one for each index of `parts`. The reference program is written for one: setup_inputs(seed, part) draws one part's arguments, and reference() takes and returns one part's arrays. A program takes and returns all parts, laid end to end along the dimension named above; an argument that names none is the same for every part. Nothing has to cross between parts.
Inputs may be any that keep to these rules, and one draw needn't show every extreme that they name: `slot_of`: A token's two slots differ; at most 64 of the choices of one block of 64 tokens name one slot, a bound that some block reaches.
All inputs are finite; a program needn't handle non-finite values.
Results may differ from the reference program's by a relative error of at most 0.007.
Values may be sent and summed in bfloat16 or wider, within the bound.
No kernel may reach another device: no remote copies, remote signals or barrier semaphores. Data moves between devices by JAX's collectives and lax.ppermute only.
A program may use at most 64 MiB of HBM per device.

```python
import math
import jax
import jax.numpy as jnp
import numpy as np
from jax import lax

D = 3072
TOK_DEV = 64
FF = 2048
TOKENS = 256
CAP = 64
N_EXPERT = 4


def shard_levels(stream_key, dims, pieces, low, largest):
    loudness, own = 1.0, jax.random.fold_in(stream_key, 6)
    for dim, parts in pieces:
        draws = jnp.exp(jax.random.uniform(jax.random.fold_in(own, dim), (parts,), jnp.float32, low / len(pieces), largest / len(pieces)))
        loudness = loudness * jnp.repeat(draws, dims[dim] // parts).reshape([-1 if axis == dim else 1 for axis in range(len(dims))])
    return loudness


def assign_block(stream_key, own, number, rows, number_of, top, most, slope):
    sequence = jax.random.permutation(stream_key, number_of)
    heavy_load, common = load_shares(number_of, rows * top, most, slope, True), load_shares(number_of, rows * top, most, slope, False)
    places = jnp.arange(number_of)

    def named(sizes, rotation):
        used = int((sizes > 0).sum())
        fixed = max(1, used // 4)
        shifted = fixed + (places - fixed + rotation * (used - fixed)) % max(1, number_of - fixed)
        return jnp.zeros((number_of,), jnp.int32).at[sequence[jnp.where(places < fixed, places, shifted)]].set(jnp.asarray(sizes, jnp.int32))

    sizes = jnp.where(number % 4 == 0, named(heavy_load, number // 4), named(common, number - number // 4 - 1))
    mixed = jax.random.permutation(jax.random.fold_in(own, 3), number_of)
    giver, sink = mixed[0:number_of // 2 * 2:2], mixed[1:number_of // 2 * 2:2]
    room = jnp.minimum(sizes[giver] - 1, most - sizes[sink]) // 2
    room = jnp.where((giver == sequence[0]) | (sink == sequence[0]) | (sizes[sink] == 0), 0, jnp.maximum(room, 0))
    shifted = jax.random.randint(jax.random.fold_in(own, 4), (number_of // 2,), 0, 1 << 20) % (room + 1)
    sizes = sizes.at[giver].add(-shifted).at[sink].add(shifted)
    members = jnp.searchsorted(jnp.cumsum(sizes), jnp.arange(rows * top), side="right").astype(jnp.int32)
    table = members.reshape(top, rows).T
    table = table[jax.random.permutation(jax.random.fold_in(own, 1), rows)]
    rotation = jax.random.randint(jax.random.fold_in(own, 2), (rows, 1), 0, top)
    return jnp.take_along_axis(table, (jnp.arange(top)[None, :] + rotation) % top, axis=1)


def load_shares(count, total, limit, skew, full):
    loads = [(1 << 20) // math.isqrt(standing ** skew) + 1 for standing in range(1, count + 1)]
    largest = limit if full else min(limit, max(-(-total // count), total * loads[0] // sum(loads)))
    least = 1 if total - largest >= count - 1 else 0
    given, spare = [largest] + [least] * (count - 1), total - largest - least * (count - 1)
    while spare > 0:
        movable = [i for i in range(1, count) if given[i] < largest] or [i for i in range(1, count) if given[i] < limit]
        mass, remaining = sum([loads[i] for i in movable]), spare
        for i in movable:
            more = min(limit - given[i], max(1, remaining * loads[i] // mass), spare)
            given[i] = given[i] + more
            spare = spare - more
    return np.array(given)


def bell_draw(stream_key, shape, scale, bound, shards=(), held_as=jnp.bfloat16):
    array = scale * jax.random.normal(stream_key, shape, jnp.float32)
    if shards:
        array = array * shard_levels(stream_key, shape, shards, -0.22, 0.18)
    return jnp.clip(array, -bound, bound).astype(held_as)


def setup_inputs(seed: int = 0, part: int = 0) -> dict:
    splits = jax.random.split(jax.random.key(seed), 7)
    part_keys = jax.random.split(jax.random.fold_in(splits[6], part), 7)
    out_grad = bell_draw(part_keys[0], (TOKENS, D), 1.0, 6.0, ((0, 4), (1, 4)))
    router_logits = bell_draw(part_keys[1], (TOKENS, 2), 1.5, 6.0, ((0, 4),), jnp.float32)
    slot_of_keys = jax.random.split(jax.random.fold_in(part_keys[2], 1), TOKENS // TOK_DEV)
    slot_of_turns = jax.random.permutation(jax.random.fold_in(part_keys[2], 3), TOKENS // TOK_DEV)
    slot_of = jax.vmap(lambda own, number: assign_block(jax.random.fold_in(part_keys[2], 2), own, number, TOK_DEV, N_EXPERT, 2, CAP, 2))(slot_of_keys, slot_of_turns).reshape((TOKENS, 2))
    gate_pre = bell_draw(part_keys[3], (N_EXPERT * N_EXPERT * CAP, FF), 1.0, 6.0, ((0, 4), (1, 4)))
    up_pre = bell_draw(part_keys[4], (N_EXPERT * N_EXPERT * CAP, FF), 1.0, 6.0, ((0, 4), (1, 4)))
    down_weight = bell_draw(splits[5], (N_EXPERT, FF, D), FF ** -0.5, 0.125, ((0, 4), (1, 4)))
    return {"out_grad": out_grad, "router_logits": router_logits, "slot_of": slot_of, "gate_pre": gate_pre, "up_pre": up_pre, "down_weight": down_weight}


def slot_product(pair):
    return jnp.dot(pair[0], pair[1].T, preferred_element_type=jnp.float32)


def reference(out_grad, router_logits, slot_of, gate_pre, up_pre, down_weight):
    first = jax.nn.sigmoid(router_logits[:, 0] - router_logits[:, 1])
    probs = jnp.stack([first, 1.0 - first], axis=1)
    probs_b = probs.astype(jnp.bfloat16)
    blocks = slot_of.reshape(N_EXPERT, TOK_DEV * 2)
    onehot = (blocks[:, :, None] == jnp.arange(N_EXPERT, dtype=jnp.int32)[None, None, :]).astype(jnp.int32)
    earlier = (jnp.cumsum(onehot, axis=1).astype(jnp.int32) - onehot) * onehot
    position = jnp.sum(earlier, axis=2).astype(jnp.int32)
    source = jnp.arange(N_EXPERT, dtype=jnp.int32)[:, None]
    dest = (blocks * (N_EXPERT * CAP) + source * CAP + position).reshape(-1).astype(jnp.int32)
    total_rows = N_EXPERT * N_EXPERT * CAP
    rows_dy = jnp.repeat(out_grad, 2, axis=0)
    received = jnp.zeros((total_rows, D), out_grad.dtype).at[dest].set(rows_dy)
    row_weight = jnp.zeros((total_rows,), probs_b.dtype).at[dest].set(probs_b.reshape(-1))
    stacked = received.reshape(N_EXPERT, N_EXPERT * CAP, D)
    z = lax.map(slot_product, (stacked, down_weight)).reshape(total_rows, FF)
    g = gate_pre.astype(jnp.float32)
    u = up_pre.astype(jnp.float32)
    sig = jax.nn.sigmoid(g)
    act = g * sig
    hb = (act * u).astype(jnp.bfloat16)
    dh = row_weight.astype(jnp.float32)[:, None] * z
    grad_up = (dh * act).astype(jnp.bfloat16)
    grad_gate = (dh * u * sig * (1.0 + g * (1.0 - sig))).astype(jnp.bfloat16)
    dp = jnp.sum(hb.astype(jnp.float32) * z, axis=1)
    picked = dp[dest].reshape(TOKENS, 2)
    mean_term = jnp.sum(probs * picked, axis=1, keepdims=True)
    logit_grad = probs * (picked - mean_term)
    return grad_gate, grad_up, logit_grad
```

```python
import jax
import jax.numpy as jnp
from jax import lax
from jax.experimental import pallas as pl
from jax.experimental.pallas import tpu as pltpu
from jax.sharding import PartitionSpec as P

BF16 = jnp.bfloat16
F32 = jnp.float32
NT = (((1,), (1,)), ((), ()))
META = 16


def vmem_specs(count):
    return [pl.BlockSpec(memory_space=pltpu.VMEM)] * count


def call(kernel, outs, args, scratch=(), flops=0, limit=16):
    out_bytes = sum(o.size * o.dtype.itemsize for o in outs)
    in_bytes = sum(a.size * a.dtype.itemsize for a in args)
    return pl.pallas_call(
        kernel,
        out_shape=tuple(outs),
        in_specs=vmem_specs(len(args)),
        out_specs=tuple(vmem_specs(len(outs))),
        scratch_shapes=list(scratch),
        compiler_params=pltpu.CompilerParams(vmem_limit_bytes=limit * 2**20),
        cost_estimate=pl.CostEstimate(
            flops=flops, bytes_accessed=out_bytes + in_bytes, transcendentals=0
        ),
    )(*args)


def pack_kernel(rows_ref, logits_ref, slots_ref, out_ref):
    tokens, width = rows_ref.shape
    first = jax.nn.sigmoid(logits_ref[0:1, :] - logits_ref[1:2, :])
    facts = jnp.concatenate(
        [
            slots_ref[...].astype(F32),
            first,
            1.0 - first,
            jnp.zeros((META - 4, tokens), F32),
        ],
        axis=0,
    )
    out_ref[:tokens, :] = rows_ref[...]
    out_ref[tokens:, :] = jnp.concatenate(
        [facts, jnp.zeros((META, width - tokens), F32)], axis=1
    ).astype(BF16)


def place_rows(target, index, blocks, mine, tokens):
    for other, block in enumerate(blocks):
        start = pl.multiple_of((mine ^ other) * tokens, tokens)
        target[index, pl.ds(start, tokens), :] = block


def first_kernel(
    own_ref, x_ref, z1_ref, d1_ref, sib_ref, weight_ref, gate_ref, up_ref,
    total_ref, hb_ref, place_ref, chosen_ref, row_weight_ref,
    rows_s, facts_s,
):
    mine, deep = lax.axis_index("expert"), lax.axis_index("etp")
    tokens, width = z1_ref.shape
    long = tokens + META
    groups = total_ref.shape[0] // tokens
    sib = (0, long, long + tokens, 2 * long + tokens)
    place_rows(
        rows_s, 0,
        (own_ref[:tokens, :], sib_ref[sib[0] : sib[0] + tokens, :], x_ref[:tokens, :], sib_ref[sib[2] : sib[2] + tokens, :]),
        mine, tokens,
    )
    place_rows(
        rows_s, 1,
        (z1_ref[...], sib_ref[sib[1] : sib[1] + tokens, :], d1_ref[...], sib_ref[sib[3] : sib[3] + tokens, :]),
        mine, tokens,
    )
    for other, (ref, start) in enumerate(
        ((own_ref, 0), (sib_ref, sib[0]), (x_ref, 0), (sib_ref, sib[2]))
    ):
        facts_s[mine ^ other] = ref[start + tokens : start + long, :tokens].astype(F32)
    total = None
    for index in range(2):
        start = pl.multiple_of((deep ^ index) * width, 128)
        part = lax.dot_general(
            rows_s[index], weight_ref[:, pl.ds(start, width)], NT, preferred_element_type=F32
        )
        total = part if total is None else total + part
    total_ref[...] = total
    g = gate_ref[...].astype(F32)
    hb_ref[...] = (g * jax.nn.sigmoid(g) * up_ref[...].astype(F32)).astype(BF16)
    slot = mine.astype(F32)
    row = lax.broadcasted_iota(jnp.int32, (tokens, tokens), 0)
    lane = lax.broadcasted_iota(jnp.int32, (tokens, tokens), 1)
    before = (row < lane).astype(BF16)
    row_f = row.astype(F32)
    firsts = [(facts_s[j, 0:1, :] == slot).astype(F32) for j in range(groups)]
    seconds = [(facts_s[j, 1:2, :] == slot).astype(F32) for j in range(groups)]
    chosen = jnp.concatenate(firsts + seconds, axis=0)
    chosen_ref[...] = chosen
    match = chosen[:groups] + chosen[groups:]
    position = jnp.dot(
        jnp.concatenate([match, match], axis=0).astype(BF16), before, preferred_element_type=F32
    )
    for j in range(groups):
        hit = (position[j : j + 1] == row_f) & (match[j : j + 1] > 0.5)
        place = hit.astype(F32)
        weight = firsts[j] * facts_s[j, 2:3, :] + seconds[j] * facts_s[j, 3:4, :]
        place_ref[j] = place
        row_weight_ref[j * tokens : (j + 1) * tokens, :] = jnp.sum(
            place * weight, axis=1, keepdims=True
        )


def second_kernel(
    total_ref, z2_ref, z3_ref, x2_ref, d3_ref, sib_a_ref, sib_b_ref, weight_ref,
    hb_ref, place_ref, chosen_ref, row_weight_ref,
    dh_ref, share_ref,
    rows_s,
):
    mine, deep = lax.axis_index("expert"), lax.axis_index("etp")
    tokens, width = z2_ref.shape
    groups = total_ref.shape[0] // tokens
    last = sib_a_ref.shape[0] - tokens
    place_rows(
        rows_s, 0,
        (z2_ref[...], sib_a_ref[last:, :], x2_ref[...], sib_b_ref[tokens : 2 * tokens, :]),
        mine, tokens,
    )
    place_rows(
        rows_s, 1,
        (z3_ref[...], sib_b_ref[:tokens, :], d3_ref[...], sib_b_ref[2 * tokens :, :]),
        mine, tokens,
    )
    total = total_ref[...]
    for index in range(2):
        start = pl.multiple_of((deep ^ (2 + index)) * width, 128)
        total = total + lax.dot_general(
            rows_s[index], weight_ref[:, pl.ds(start, width)], NT, preferred_element_type=F32
        )
    sums = []
    for j in range(groups):
        part = slice(j * tokens, (j + 1) * tokens)
        place = place_ref[j]
        place_b = place.astype(BF16)
        high = total[part].astype(BF16)
        low = (total[part] - high.astype(F32)).astype(BF16)
        z = jnp.dot(place_b, high, preferred_element_type=F32) + jnp.dot(
            place_b, low, preferred_element_type=F32
        )
        dh_ref[part, :] = row_weight_ref[part, :] * z
        dp = jnp.sum(hb_ref[part, :].astype(F32) * z, axis=1, keepdims=True)
        sums.append(jnp.sum(place * dp, axis=0, keepdims=True))
    sums = jnp.concatenate(sums, axis=0)
    share_ref[...] = chosen_ref[...] * jnp.concatenate([sums, sums], axis=0)


def grads_kernel(dh_ref, gate_ref, up_ref, grad_gate_ref, grad_up_ref):
    g = gate_ref[...].astype(F32)
    u = up_ref[...].astype(F32)
    dh = dh_ref[...]
    sig = jax.nn.sigmoid(g)
    grad_up_ref[...] = (dh * (g * sig)).astype(BF16)
    grad_gate_ref[...] = (dh * u * sig * (1.0 + g * (1.0 - sig))).astype(BF16)


def logits_kernel(a_ref, b_ref, c_ref, d_ref, logits_ref, out_ref, sum_s):
    mine = lax.axis_index("expert")
    groups = a_ref.shape[0] // 2
    sum_s[...] = (a_ref[...] + b_ref[...]) + (c_ref[...] + d_ref[...])
    picked_0 = sum_s[pl.ds(mine, 1), :]
    picked_1 = sum_s[pl.ds(mine + groups, 1), :]
    first = jax.nn.sigmoid(logits_ref[0:1, :] - logits_ref[1:2, :])
    second = 1.0 - first
    mean = first * picked_0 + second * picked_1
    out_ref[...] = jnp.concatenate([first * (picked_0 - mean), second * (picked_1 - mean)], axis=0)


def small_body(out_grad, router_logits, slot_of, gate_pre, up_pre, down_weight):
    tokens, width = out_grad.shape
    rows, hidden = gate_pre.shape
    weight = down_weight[0]
    slots, deep = lax.axis_size("expert"), lax.axis_size("etp")

    def swap(value, dx, dc, dz):
        mask = (dx * 2 + dc) * deep + dz
        return lax.ppermute(
            value, ("expert", "etp"), [(i, i ^ mask) for i in range(slots * deep)]
        )

    logits_t, slots_t = router_logits.T, slot_of.T
    (own,) = call(
        pack_kernel,
        [jax.ShapeDtypeStruct((tokens + META, width), BF16)],
        [out_grad, logits_t, slots_t],
    )
    z2 = swap(out_grad, 0, 0, 2)
    z1 = swap(out_grad, 0, 0, 1)
    xo = swap(own, 1, 0, 0)
    d1 = swap(out_grad, 1, 0, 1)
    z3 = swap(z2, 0, 0, 1)
    x2 = swap(z2, 1, 0, 0)
    d3 = swap(z2, 1, 0, 1)
    sib_a = swap(jnp.concatenate([own, z1, xo, d1, z2], axis=0), 0, 1, 0)
    sib_b = swap(jnp.concatenate([z3, x2, d3], axis=0), 0, 1, 0)
    half_flops = 2 * rows * hidden * width * 2
    total, hb, place, chosen, row_weight = call(
        first_kernel,
        [
            jax.ShapeDtypeStruct((rows, hidden), F32),
            jax.ShapeDtypeStruct((rows, hidden), BF16),
            jax.ShapeDtypeStruct((slots, tokens, tokens), F32),
            jax.ShapeDtypeStruct((2 * slots, tokens), F32),
            jax.ShapeDtypeStruct((rows, 1), F32),
        ],
        [own, xo, z1, d1, sib_a, weight, gate_pre, up_pre],
        scratch=[pltpu.VMEM((2, rows, width), BF16), pltpu.VMEM((slots, META, tokens), F32)],
        flops=half_flops,
    )
    dh, share = call(
        second_kernel,
        [
            jax.ShapeDtypeStruct((rows, hidden), F32),
            jax.ShapeDtypeStruct((2 * slots, tokens), F32),
        ],
        [total, z2, z3, x2, d3, sib_a, sib_b, weight, hb, place, chosen, row_weight],
        scratch=[pltpu.VMEM((2, rows, width), BF16)],
        flops=half_flops,
    )
    share = share + swap(share, 0, 1, 0) + swap(share, 1, 0, 0) + swap(share, 1, 1, 0)
    pieces = [share] + [swap(share, 0, 0, dz) for dz in range(1, deep)]
    grad_gate, grad_up = call(
        grads_kernel,
        [jax.ShapeDtypeStruct((rows, hidden), BF16)] * 2,
        [dh, gate_pre, up_pre],
    )
    (logit_grad,) = call(
        logits_kernel,
        [jax.ShapeDtypeStruct((2, tokens), F32)],
        [*pieces, logits_t],
        scratch=[pltpu.VMEM((2 * slots, tokens), F32)],
    )
    return grad_gate, grad_up, logit_grad.T


def body(out_grad, router_logits, slot_of, gate_pre, up_pre, down_weight):
    slots = lax.axis_size("expert")
    total_rows = gate_pre.shape[0]
    capacity = total_rows // slots
    weight = down_weight[0]
    first = jax.nn.sigmoid(router_logits[:, 0] - router_logits[:, 1])
    probs = jnp.stack([first, 1.0 - first], axis=1)
    probs_b = probs.astype(jnp.bfloat16)
    flat_slot = slot_of.reshape(-1)
    onehot = (flat_slot[:, None] == jnp.arange(slots, dtype=jnp.int32)[None, :]).astype(jnp.int32)
    earlier = (jnp.cumsum(onehot, axis=0) - onehot) * onehot
    position = jnp.sum(earlier, axis=1)
    dest = flat_slot * capacity + position
    placing = dest[:, None] == jnp.arange(total_rows, dtype=jnp.int32)[None, :]
    place_b = placing.astype(jnp.bfloat16)
    place_f = placing.astype(jnp.float32)
    rows_dy = jnp.repeat(out_grad, 2, axis=0)
    send_rows = lax.dot_general(
        place_b, rows_dy, (((0,), (0,)), ((), ())), preferred_element_type=jnp.float32
    ).astype(jnp.bfloat16)
    send_weight = jnp.dot(probs_b.reshape(-1).astype(jnp.float32), place_f).astype(jnp.bfloat16)
    received, row_weight = (
        lax.all_to_all(send_rows, "expert", split_axis=0, concat_axis=0, tiled=True),
        lax.all_to_all(send_weight, "expert", split_axis=0, concat_axis=0, tiled=True),
    )
    z_local = lax.dot_general(
        lax.all_gather(received, "etp", axis=1, tiled=True),
        weight,
        (((1,), (1,)), ((), ())),
        preferred_element_type=jnp.float32,
    )
    g = gate_pre.astype(jnp.float32)
    u = up_pre.astype(jnp.float32)
    sig = jax.nn.sigmoid(g)
    act = g * sig
    hb = (act * u).astype(jnp.bfloat16)
    dh = row_weight.astype(jnp.float32)[:, None] * z_local
    grad_up = (dh * act).astype(jnp.bfloat16)
    grad_gate = (dh * u * sig * (1.0 + g * (1.0 - sig))).astype(jnp.bfloat16)
    partial_dp = jnp.sum(hb.astype(jnp.float32) * z_local, axis=1)
    row_dp = lax.psum(partial_dp, "etp")
    returned = lax.all_to_all(row_dp, "expert", split_axis=0, concat_axis=0, tiled=True)
    picked = jnp.dot(place_f, returned).reshape(probs.shape)
    mean_term = jnp.sum(probs * picked, axis=1, keepdims=True)
    logit_grad = probs * (picked - mean_term)
    return (grad_gate, grad_up, logit_grad)


def solution(mesh):
    small = mesh.shape["expert"] == 4 and mesh.shape["etp"] == 4
    return jax.shard_map(
        small_body if small else body,
        mesh=mesh,
        in_specs=(
            P(("parts", "expert"), "etp"),
            P(("parts", "expert"), None),
            P(("parts", "expert"), None),
            P(("parts", "expert"), "etp"),
            P(("parts", "expert"), "etp"),
            P("expert", "etp", None),
        ),
        out_specs=(
            P(("parts", "expert"), "etp"),
            P(("parts", "expert"), "etp"),
            P(("parts", "expert"), None),
        ),
        check_vma=False,
    )
```

```python
import jax
import jax.numpy as jnp
from jax import lax
from jax.experimental import pallas as pl
from jax.experimental.pallas import tpu as pltpu
from jax.sharding import PartitionSpec as P

BF16 = jnp.bfloat16
F32 = jnp.float32
NT = (((1,), (1,)), ((), ()))
META = 16


VMEM = pl.BlockSpec(memory_space=pltpu.VMEM)
HBM = pl.BlockSpec(memory_space=pltpu.HBM)


def call(kernel, outs, args, scratch=(), flops=0, limit=16, hbm=0):
    args = [pltpu.with_memory_space_constraint(a, pltpu.HBM) for a in args[:hbm]] + list(args[hbm:])
    out_bytes = sum(o.size * o.dtype.itemsize for o in outs)
    in_bytes = sum(a.size * a.dtype.itemsize for a in args)
    return pl.pallas_call(
        kernel,
        out_shape=tuple(outs),
        in_specs=[HBM] * hbm + [VMEM] * (len(args) - hbm),
        out_specs=tuple([VMEM] * len(outs)),
        scratch_shapes=list(scratch),
        compiler_params=pltpu.CompilerParams(vmem_limit_bytes=limit * 2**20),
        cost_estimate=pl.CostEstimate(
            flops=flops, bytes_accessed=out_bytes + in_bytes, transcendentals=0
        ),
    )(*args)


def facts_kernel(logits_hbm, slots_hbm, out_ref, logits_ref, slots_ref, sems):
    meta, width = out_ref.shape
    tokens = logits_ref.shape[1]
    copies = [
        pltpu.make_async_copy(logits_hbm, logits_ref, sems.at[0]),
        pltpu.make_async_copy(slots_hbm, slots_ref, sems.at[1]),
    ]
    for copy in copies:
        copy.start()
    for copy in copies:
        copy.wait()
    first = jax.nn.sigmoid(logits_ref[0:1, :] - logits_ref[1:2, :])
    facts = jnp.concatenate(
        [slots_ref[...].astype(F32), first, 1.0 - first, jnp.zeros((meta - 4, tokens), F32)],
        axis=0,
    )
    out_ref[...] = jnp.concatenate(
        [facts, jnp.zeros((meta, width - tokens), F32)], axis=1
    ).astype(BF16)


def load_kernel(
    weight_hbm, gate_hbm, up_hbm, rows_hbm, facts_ref,
    weight_ref, gate_ref, up_ref, hb_ref, own_ref,
    sems,
):
    tokens = rows_hbm.shape[0]
    copies = [
        pltpu.make_async_copy(gate_hbm, gate_ref, sems.at[0]),
        pltpu.make_async_copy(up_hbm, up_ref, sems.at[1]),
        pltpu.make_async_copy(weight_hbm, weight_ref, sems.at[2]),
        pltpu.make_async_copy(rows_hbm, own_ref.at[pl.ds(0, tokens)], sems.at[3]),
    ]
    for copy in copies:
        copy.start()
    own_ref[tokens:, :] = facts_ref[...]
    copies[0].wait()
    copies[1].wait()
    g = gate_ref[...].astype(F32)
    hb_ref[...] = (g * jax.nn.sigmoid(g) * up_ref[...].astype(F32)).astype(BF16)
    copies[2].wait()
    copies[3].wait()


def bundle_kernel(a_ref, b_ref, c_ref, order_ref, out_ref):
    tokens = a_ref.shape[0]
    out_ref[:tokens, :] = a_ref[...]
    out_ref[tokens : 2 * tokens, :] = b_ref[...]
    out_ref[2 * tokens :, :] = c_ref[...]


def place_rows(target, index, blocks, mine, tokens):
    for other, block in enumerate(blocks):
        start = pl.multiple_of((mine ^ other) * tokens, tokens)
        target[index, pl.ds(start, tokens), :] = block


def first_kernel(
    own_ref, x_facts_ref, x_ref, z1_ref, d1_ref, sib_ref, weight_ref,
    total_ref, place_ref, chosen_ref, row_weight_ref,
    rows_s, facts_s,
):
    mine, deep = lax.axis_index("expert"), lax.axis_index("etp")
    tokens, width = z1_ref.shape
    long = tokens + META
    groups = total_ref.shape[0] // tokens
    sib_z1 = long + META
    sib_x = sib_z1 + tokens
    sib_d1 = sib_x + tokens
    place_rows(
        rows_s, 0,
        (own_ref[:tokens, :], sib_ref[:tokens, :], x_ref[...], sib_ref[sib_x:sib_d1, :]),
        mine, tokens,
    )
    place_rows(
        rows_s, 1,
        (z1_ref[...], sib_ref[sib_z1:sib_x, :], d1_ref[...], sib_ref[sib_d1 : sib_d1 + tokens, :]),
        mine, tokens,
    )
    for other, (ref, start) in enumerate(
        ((own_ref, tokens), (sib_ref, tokens), (x_facts_ref, 0), (sib_ref, long))
    ):
        facts_s[mine ^ other] = ref[start : start + META, :tokens].astype(F32)
    total = None
    for index in range(2):
        start = pl.multiple_of((deep ^ index) * width, 128)
        part = lax.dot_general(
            rows_s[index], weight_ref[:, pl.ds(start, width)], NT, preferred_element_type=F32
        )
        total = part if total is None else total + part
    total_ref[...] = total
    slot = mine.astype(F32)
    row = lax.broadcasted_iota(jnp.int32, (tokens, tokens), 0)
    lane = lax.broadcasted_iota(jnp.int32, (tokens, tokens), 1)
    before = (row < lane).astype(BF16)
    row_f = row.astype(F32)
    firsts = [(facts_s[j, 0:1, :] == slot).astype(F32) for j in range(groups)]
    seconds = [(facts_s[j, 1:2, :] == slot).astype(F32) for j in range(groups)]
    chosen = jnp.concatenate(firsts + seconds, axis=0)
    chosen_ref[...] = chosen
    match = chosen[:groups] + chosen[groups:]
    position = jnp.dot(
        jnp.concatenate([match, match], axis=0).astype(BF16), before, preferred_element_type=F32
    )
    for j in range(groups):
        hit = (position[j : j + 1] == row_f) & (match[j : j + 1] > 0.5)
        place = hit.astype(F32)
        weight = firsts[j] * facts_s[j, 2:3, :] + seconds[j] * facts_s[j, 3:4, :]
        place_ref[j] = place
        row_weight_ref[j * tokens : (j + 1) * tokens, :] = jnp.sum(
            place * weight, axis=1, keepdims=True
        )


def second_kernel(
    total_ref, z2_ref, z3_ref, x2_ref, d3_ref, sib_a_ref, sib_b_ref, weight_ref,
    hb_ref, place_ref, chosen_ref, row_weight_ref,
    dh_ref, share_ref,
    rows_s,
):
    mine, deep = lax.axis_index("expert"), lax.axis_index("etp")
    tokens, width = z2_ref.shape
    groups = total_ref.shape[0] // tokens
    last = sib_a_ref.shape[0] - tokens
    place_rows(
        rows_s, 0,
        (z2_ref[...], sib_a_ref[last:, :], x2_ref[...], sib_b_ref[tokens : 2 * tokens, :]),
        mine, tokens,
    )
    place_rows(
        rows_s, 1,
        (z3_ref[...], sib_b_ref[:tokens, :], d3_ref[...], sib_b_ref[2 * tokens :, :]),
        mine, tokens,
    )
    total = total_ref[...]
    for index in range(2):
        start = pl.multiple_of((deep ^ (2 + index)) * width, 128)
        total = total + lax.dot_general(
            rows_s[index], weight_ref[:, pl.ds(start, width)], NT, preferred_element_type=F32
        )
    sums = []
    for j in range(groups):
        part = slice(j * tokens, (j + 1) * tokens)
        place = place_ref[j]
        place_b = place.astype(BF16)
        high = total[part].astype(BF16)
        low = (total[part] - high.astype(F32)).astype(BF16)
        z = jnp.dot(place_b, high, preferred_element_type=F32) + jnp.dot(
            place_b, low, preferred_element_type=F32
        )
        dh_ref[part, :] = row_weight_ref[part, :] * z
        dp = jnp.sum(hb_ref[part, :].astype(F32) * z, axis=1, keepdims=True)
        sums.append(jnp.sum(place * dp, axis=0, keepdims=True))
    sums = jnp.concatenate(sums, axis=0)
    share_ref[...] = chosen_ref[...] * jnp.concatenate([sums, sums], axis=0)


def grads_kernel(dh_ref, gate_ref, up_ref, grad_gate_ref, grad_up_ref):
    g = gate_ref[...].astype(F32)
    u = up_ref[...].astype(F32)
    dh = dh_ref[...]
    sig = jax.nn.sigmoid(g)
    grad_up_ref[...] = (dh * (g * sig)).astype(BF16)
    grad_gate_ref[...] = (dh * u * sig * (1.0 + g * (1.0 - sig))).astype(BF16)


def logits_kernel(a_ref, b_ref, c_ref, d_ref, logits_ref, out_ref, sum_s):
    mine = lax.axis_index("expert")
    groups = a_ref.shape[0] // 2
    sum_s[...] = (a_ref[...] + b_ref[...]) + (c_ref[...] + d_ref[...])
    picked_0 = sum_s[pl.ds(mine, 1), :]
    picked_1 = sum_s[pl.ds(mine + groups, 1), :]
    first = jax.nn.sigmoid(logits_ref[0:1, :] - logits_ref[1:2, :])
    second = 1.0 - first
    mean = first * picked_0 + second * picked_1
    out_ref[...] = jnp.concatenate([first * (picked_0 - mean), second * (picked_1 - mean)], axis=0)


def small_body(out_grad, router_logits, slot_of, gate_pre, up_pre, down_weight):
    tokens, width = out_grad.shape
    rows, hidden = gate_pre.shape
    weight = down_weight[0]
    slots, deep = lax.axis_size("expert"), lax.axis_size("etp")

    def swap(value, dx, dc, dz):
        mask = (dx * 2 + dc) * deep + dz
        return lax.ppermute(
            value, ("expert", "etp"), [(i, i ^ mask) for i in range(slots * deep)]
        )

    logits_t, slots_t = router_logits.T, slot_of.T
    z2 = swap(out_grad, 0, 0, 2)
    z1 = swap(out_grad, 0, 0, 1)
    xo = swap(out_grad, 1, 0, 0)
    d1 = swap(out_grad, 1, 0, 1)
    (facts,) = call(
        facts_kernel,
        [jax.ShapeDtypeStruct((META, width), BF16)],
        [logits_t, slots_t],
        scratch=[
            pltpu.VMEM((2, tokens), F32),
            pltpu.VMEM((2, tokens), jnp.int32),
            pltpu.SemaphoreType.DMA((2,)),
        ],
        hbm=2,
    )
    x_facts = swap(facts, 1, 0, 0)
    weight, gate, up, hb, own = call(
        load_kernel,
        [
            jax.ShapeDtypeStruct(weight.shape, BF16),
            jax.ShapeDtypeStruct((rows, hidden), BF16),
            jax.ShapeDtypeStruct((rows, hidden), BF16),
            jax.ShapeDtypeStruct((rows, hidden), BF16),
            jax.ShapeDtypeStruct((tokens + META, width), BF16),
        ],
        [weight, gate_pre, up_pre, out_grad, facts],
        scratch=[pltpu.SemaphoreType.DMA((4,))],
        hbm=4,
    )
    z3 = swap(z2, 0, 0, 1)
    x2 = swap(z2, 1, 0, 0)
    d3 = swap(z2, 1, 0, 1)
    sib_a = swap(jnp.concatenate([own, x_facts, z1, xo, d1, z2], axis=0), 0, 1, 0)
    half_flops = 2 * rows * hidden * width * 2
    total, place, chosen, row_weight = call(
        first_kernel,
        [
            jax.ShapeDtypeStruct((rows, hidden), F32),
            jax.ShapeDtypeStruct((slots, tokens, tokens), F32),
            jax.ShapeDtypeStruct((2 * slots, tokens), F32),
            jax.ShapeDtypeStruct((rows, 1), F32),
        ],
        [own, x_facts, xo, z1, d1, sib_a, weight],
        scratch=[pltpu.VMEM((2, rows, width), BF16), pltpu.VMEM((slots, META, tokens), F32)],
        flops=half_flops,
    )
    (bundle,) = call(
        bundle_kernel,
        [jax.ShapeDtypeStruct((3 * tokens, width), BF16)],
        [z3, x2, d3, chosen],
    )
    sib_b = swap(bundle, 0, 1, 0)
    dh, share = call(
        second_kernel,
        [
            jax.ShapeDtypeStruct((rows, hidden), F32),
            jax.ShapeDtypeStruct((2 * slots, tokens), F32),
        ],
        [total, z2, z3, x2, d3, sib_a, sib_b, weight, hb, place, chosen, row_weight],
        scratch=[pltpu.VMEM((2, rows, width), BF16)],
        flops=half_flops,
    )
    share = share + swap(share, 0, 1, 0) + swap(share, 1, 0, 0) + swap(share, 1, 1, 0)
    pieces = [share] + [swap(share, 0, 0, dz) for dz in range(1, deep)]
    grad_gate, grad_up = call(
        grads_kernel,
        [jax.ShapeDtypeStruct((rows, hidden), BF16)] * 2,
        [dh, gate, up],
    )
    (logit_grad,) = call(
        logits_kernel,
        [jax.ShapeDtypeStruct((2, tokens), F32)],
        [*pieces, logits_t],
        scratch=[pltpu.VMEM((2 * slots, tokens), F32)],
    )
    return grad_gate, grad_up, logit_grad.T


def body(out_grad, router_logits, slot_of, gate_pre, up_pre, down_weight):
    slots = lax.axis_size("expert")
    total_rows = gate_pre.shape[0]
    capacity = total_rows // slots
    weight = down_weight[0]
    first = jax.nn.sigmoid(router_logits[:, 0] - router_logits[:, 1])
    probs = jnp.stack([first, 1.0 - first], axis=1)
    probs_b = probs.astype(jnp.bfloat16)
    flat_slot = slot_of.reshape(-1)
    onehot = (flat_slot[:, None] == jnp.arange(slots, dtype=jnp.int32)[None, :]).astype(jnp.int32)
    earlier = (jnp.cumsum(onehot, axis=0) - onehot) * onehot
    position = jnp.sum(earlier, axis=1)
    dest = flat_slot * capacity + position
    placing = dest[:, None] == jnp.arange(total_rows, dtype=jnp.int32)[None, :]
    place_b = placing.astype(jnp.bfloat16)
    place_f = placing.astype(jnp.float32)
    rows_dy = jnp.repeat(out_grad, 2, axis=0)
    send_rows = lax.dot_general(
        place_b, rows_dy, (((0,), (0,)), ((), ())), preferred_element_type=jnp.float32
    ).astype(jnp.bfloat16)
    send_weight = jnp.dot(probs_b.reshape(-1).astype(jnp.float32), place_f).astype(jnp.bfloat16)
    received, row_weight = (
        lax.all_to_all(send_rows, "expert", split_axis=0, concat_axis=0, tiled=True),
        lax.all_to_all(send_weight, "expert", split_axis=0, concat_axis=0, tiled=True),
    )
    z_local = lax.dot_general(
        lax.all_gather(received, "etp", axis=1, tiled=True),
        weight,
        (((1,), (1,)), ((), ())),
        preferred_element_type=jnp.float32,
    )
    g = gate_pre.astype(jnp.float32)
    u = up_pre.astype(jnp.float32)
    sig = jax.nn.sigmoid(g)
    act = g * sig
    hb = (act * u).astype(jnp.bfloat16)
    dh = row_weight.astype(jnp.float32)[:, None] * z_local
    grad_up = (dh * act).astype(jnp.bfloat16)
    grad_gate = (dh * u * sig * (1.0 + g * (1.0 - sig))).astype(jnp.bfloat16)
    partial_dp = jnp.sum(hb.astype(jnp.float32) * z_local, axis=1)
    row_dp = lax.psum(partial_dp, "etp")
    returned = lax.all_to_all(row_dp, "expert", split_axis=0, concat_axis=0, tiled=True)
    picked = jnp.dot(place_f, returned).reshape(probs.shape)
    mean_term = jnp.sum(probs * picked, axis=1, keepdims=True)
    logit_grad = probs * (picked - mean_term)
    return (grad_gate, grad_up, logit_grad)


def solution(mesh):
    small = mesh.shape["expert"] == 4 and mesh.shape["etp"] == 4
    return jax.shard_map(
        small_body if small else body,
        mesh=mesh,
        in_specs=(
            P(("parts", "expert"), "etp"),
            P(("parts", "expert"), None),
            P(("parts", "expert"), None),
            P(("parts", "expert"), "etp"),
            P(("parts", "expert"), "etp"),
            P("expert", "etp", None),
        ),
        out_specs=(
            P(("parts", "expert"), "etp"),
            P(("parts", "expert"), "etp"),
            P(("parts", "expert"), None),
        ),
        check_vma=False,
    )
```

```python
import jax
import jax.numpy as jnp
from jax import lax
from jax.experimental import pallas as pl
from jax.experimental.pallas import tpu as pltpu
from jax.sharding import PartitionSpec as P

BF16 = jnp.bfloat16
F32 = jnp.float32
NT = (((1,), (1,)), ((), ()))
META = 16


VMEM = pl.BlockSpec(memory_space=pltpu.VMEM)
HBM = pl.BlockSpec(memory_space=pltpu.HBM)


def call(kernel, outs, args, scratch=(), flops=0, limit=16, hbm=0):
    args = [pltpu.with_memory_space_constraint(a, pltpu.HBM) for a in args[:hbm]] + list(args[hbm:])
    out_bytes = sum(o.size * o.dtype.itemsize for o in outs)
    in_bytes = sum(a.size * a.dtype.itemsize for a in args)
    return pl.pallas_call(
        kernel,
        out_shape=tuple(outs),
        in_specs=[HBM] * hbm + [VMEM] * (len(args) - hbm),
        out_specs=tuple([VMEM] * len(outs)),
        scratch_shapes=list(scratch),
        compiler_params=pltpu.CompilerParams(vmem_limit_bytes=limit * 2**20),
        cost_estimate=pl.CostEstimate(
            flops=flops, bytes_accessed=out_bytes + in_bytes, transcendentals=0
        ),
    )(*args)


def facts_kernel(logits_hbm, slots_hbm, out_ref, logits_ref, slots_ref, sems):
    meta, width = out_ref.shape
    tokens = logits_ref.shape[1]
    copies = [
        pltpu.make_async_copy(logits_hbm, logits_ref, sems.at[0]),
        pltpu.make_async_copy(slots_hbm, slots_ref, sems.at[1]),
    ]
    for copy in copies:
        copy.start()
    for copy in copies:
        copy.wait()
    first = jax.nn.sigmoid(logits_ref[0:1, :] - logits_ref[1:2, :])
    facts = jnp.concatenate(
        [slots_ref[...].astype(F32), first, 1.0 - first, jnp.zeros((meta - 4, tokens), F32)],
        axis=0,
    )
    out_ref[...] = jnp.concatenate(
        [facts, jnp.zeros((meta, width - tokens), F32)], axis=1
    ).astype(BF16)


def load_kernel(
    weight_hbm, gate_hbm, up_hbm, rows_hbm, facts_ref,
    weight_ref, gate_ref, up_ref, hb_ref, own_ref,
    sems,
):
    tokens = rows_hbm.shape[0]
    copies = [
        pltpu.make_async_copy(gate_hbm, gate_ref, sems.at[0]),
        pltpu.make_async_copy(up_hbm, up_ref, sems.at[1]),
        pltpu.make_async_copy(weight_hbm, weight_ref, sems.at[2]),
        pltpu.make_async_copy(rows_hbm, own_ref.at[pl.ds(0, tokens)], sems.at[3]),
    ]
    for copy in copies:
        copy.start()
    own_ref[tokens:, :] = facts_ref[...]
    copies[0].wait()
    copies[1].wait()
    g = gate_ref[...].astype(F32)
    hb_ref[...] = (g * jax.nn.sigmoid(g) * up_ref[...].astype(F32)).astype(BF16)
    copies[2].wait()
    copies[3].wait()


def bundle_kernel(a_ref, b_ref, c_ref, out_ref):
    tokens = a_ref.shape[0]
    out_ref[:tokens, :] = a_ref[...]
    out_ref[tokens : 2 * tokens, :] = b_ref[...]
    out_ref[2 * tokens :, :] = c_ref[...]


def place_rows(target, index, blocks, mine, tokens):
    for other, block in enumerate(blocks):
        start = pl.multiple_of((mine ^ other) * tokens, tokens)
        target[index, pl.ds(start, tokens), :] = block


def first_kernel(
    own_ref, x_facts_ref, x_ref, z1_ref, d1_ref, sib_ref, weight_ref,
    total_ref, place_ref, chosen_ref, row_weight_ref,
    rows_s, facts_s,
):
    mine, deep = lax.axis_index("expert"), lax.axis_index("etp")
    tokens, width = z1_ref.shape
    long = tokens + META
    groups = total_ref.shape[0] // tokens
    sib_d1 = long + tokens
    sib_x = sib_d1 + tokens
    sib_z1 = sib_x + tokens
    sib_facts = sib_z1 + tokens
    place_rows(
        rows_s, 0,
        (own_ref[:tokens, :], sib_ref[:tokens, :], x_ref[...], sib_ref[sib_x : sib_x + tokens, :]),
        mine, tokens,
    )
    place_rows(
        rows_s, 1,
        (z1_ref[...], sib_ref[sib_z1 : sib_z1 + tokens, :], d1_ref[...], sib_ref[sib_d1 : sib_d1 + tokens, :]),
        mine, tokens,
    )
    for other, (ref, start) in enumerate(
        ((own_ref, tokens), (sib_ref, tokens), (x_facts_ref, 0), (sib_ref, sib_facts))
    ):
        facts_s[mine ^ other] = ref[start : start + META, :tokens].astype(F32)
    total = None
    for index in range(2):
        start = pl.multiple_of((deep ^ index) * width, 128)
        part = lax.dot_general(
            rows_s[index], weight_ref[:, pl.ds(start, width)], NT, preferred_element_type=F32
        )
        total = part if total is None else total + part
    total_ref[...] = total
    slot = mine.astype(F32)
    row = lax.broadcasted_iota(jnp.int32, (tokens, tokens), 0)
    lane = lax.broadcasted_iota(jnp.int32, (tokens, tokens), 1)
    before = (row < lane).astype(BF16)
    row_f = row.astype(F32)
    firsts = [(facts_s[j, 0:1, :] == slot).astype(F32) for j in range(groups)]
    seconds = [(facts_s[j, 1:2, :] == slot).astype(F32) for j in range(groups)]
    chosen = jnp.concatenate(firsts + seconds, axis=0)
    chosen_ref[...] = chosen
    match = chosen[:groups] + chosen[groups:]
    position = jnp.dot(
        jnp.concatenate([match, match], axis=0).astype(BF16), before, preferred_element_type=F32
    )
    for j in range(groups):
        hit = (position[j : j + 1] == row_f) & (match[j : j + 1] > 0.5)
        place = hit.astype(F32)
        weight = firsts[j] * facts_s[j, 2:3, :] + seconds[j] * facts_s[j, 3:4, :]
        place_ref[j] = place
        row_weight_ref[j * tokens : (j + 1) * tokens, :] = jnp.sum(
            place * weight, axis=1, keepdims=True
        )


def second_kernel(
    total_ref, z2_ref, z3_ref, x2_ref, d3_ref, sib_a_ref, sib_b_ref, weight_ref,
    hb_ref, place_ref, chosen_ref, row_weight_ref,
    dh_ref, share_ref,
    rows_s,
):
    mine, deep = lax.axis_index("expert"), lax.axis_index("etp")
    tokens, width = z2_ref.shape
    groups = total_ref.shape[0] // tokens
    first = tokens + META
    place_rows(
        rows_s, 0,
        (z2_ref[...], sib_a_ref[first : first + tokens, :], x2_ref[...], sib_b_ref[tokens : 2 * tokens, :]),
        mine, tokens,
    )
    place_rows(
        rows_s, 1,
        (z3_ref[...], sib_b_ref[:tokens, :], d3_ref[...], sib_b_ref[2 * tokens :, :]),
        mine, tokens,
    )
    total = total_ref[...]
    for index in range(2):
        start = pl.multiple_of((deep ^ (2 + index)) * width, 128)
        total = total + lax.dot_general(
            rows_s[index], weight_ref[:, pl.ds(start, width)], NT, preferred_element_type=F32
        )
    sums = []
    for j in range(groups):
        part = slice(j * tokens, (j + 1) * tokens)
        place = place_ref[j]
        place_b = place.astype(BF16)
        high = total[part].astype(BF16)
        low = (total[part] - high.astype(F32)).astype(BF16)
        z = jnp.dot(place_b, high, preferred_element_type=F32) + jnp.dot(
            place_b, low, preferred_element_type=F32
        )
        dh_ref[part, :] = row_weight_ref[part, :] * z
        dp = jnp.sum(hb_ref[part, :].astype(F32) * z, axis=1, keepdims=True)
        sums.append(jnp.sum(place * dp, axis=0, keepdims=True))
    sums = jnp.concatenate(sums, axis=0)
    share_ref[...] = chosen_ref[...] * jnp.concatenate([sums, sums], axis=0)


def grads_kernel(dh_ref, gate_ref, up_ref, grad_gate_ref, grad_up_ref):
    g = gate_ref[...].astype(F32)
    u = up_ref[...].astype(F32)
    dh = dh_ref[...]
    sig = jax.nn.sigmoid(g)
    grad_up_ref[...] = (dh * (g * sig)).astype(BF16)
    grad_gate_ref[...] = (dh * u * sig * (1.0 + g * (1.0 - sig))).astype(BF16)


def logits_kernel(a_ref, b_ref, c_ref, d_ref, logits_ref, out_ref, sum_s):
    mine = lax.axis_index("expert")
    groups = a_ref.shape[0] // 2
    sum_s[...] = (a_ref[...] + b_ref[...]) + (c_ref[...] + d_ref[...])
    picked_0 = sum_s[pl.ds(mine, 1), :]
    picked_1 = sum_s[pl.ds(mine + groups, 1), :]
    first = jax.nn.sigmoid(logits_ref[0:1, :] - logits_ref[1:2, :])
    second = 1.0 - first
    mean = first * picked_0 + second * picked_1
    out_ref[...] = jnp.concatenate([first * (picked_0 - mean), second * (picked_1 - mean)], axis=0)


def small_body(out_grad, router_logits, slot_of, gate_pre, up_pre, down_weight):
    tokens, width = out_grad.shape
    rows, hidden = gate_pre.shape
    weight = down_weight[0]
    slots, deep = lax.axis_size("expert"), lax.axis_size("etp")

    def swap(value, dx, dc, dz):
        mask = (dx * 2 + dc) * deep + dz
        return lax.ppermute(
            value, ("expert", "etp"), [(i, i ^ mask) for i in range(slots * deep)]
        )

    logits_t, slots_t = router_logits.T, slot_of.T
    z2 = swap(out_grad, 0, 0, 2)
    z1 = swap(out_grad, 0, 0, 1)
    xo = swap(out_grad, 1, 0, 0)
    d1 = swap(out_grad, 1, 0, 1)
    (facts,) = call(
        facts_kernel,
        [jax.ShapeDtypeStruct((META, width), BF16)],
        [logits_t, slots_t],
        scratch=[
            pltpu.VMEM((2, tokens), F32),
            pltpu.VMEM((2, tokens), jnp.int32),
            pltpu.SemaphoreType.DMA((2,)),
        ],
        hbm=2,
    )
    x_facts = swap(facts, 1, 0, 0)
    weight, gate, up, hb, own = call(
        load_kernel,
        [
            jax.ShapeDtypeStruct(weight.shape, BF16),
            jax.ShapeDtypeStruct((rows, hidden), BF16),
            jax.ShapeDtypeStruct((rows, hidden), BF16),
            jax.ShapeDtypeStruct((rows, hidden), BF16),
            jax.ShapeDtypeStruct((tokens + META, width), BF16),
        ],
        [weight, gate_pre, up_pre, out_grad, facts],
        scratch=[pltpu.SemaphoreType.DMA((4,))],
        hbm=4,
    )
    z3 = swap(z2, 0, 0, 1)
    x2 = swap(z2, 1, 0, 0)
    d3 = swap(z2, 1, 0, 1)
    sib_a = swap(jnp.concatenate([own, z2, d1, xo, z1, x_facts], axis=0), 0, 1, 0)
    half_flops = 2 * rows * hidden * width * 2
    total, place, chosen, row_weight = call(
        first_kernel,
        [
            jax.ShapeDtypeStruct((rows, hidden), F32),
            jax.ShapeDtypeStruct((slots, tokens, tokens), F32),
            jax.ShapeDtypeStruct((2 * slots, tokens), F32),
            jax.ShapeDtypeStruct((rows, 1), F32),
        ],
        [own, x_facts, xo, z1, d1, sib_a, weight],
        scratch=[pltpu.VMEM((2, rows, width), BF16), pltpu.VMEM((slots, META, tokens), F32)],
        flops=half_flops,
    )
    (bundle,) = call(
        bundle_kernel,
        [jax.ShapeDtypeStruct((3 * tokens, width), BF16)],
        [z3, x2, d3],
        flops=4 * 10**9,
    )
    sib_b = swap(bundle, 0, 1, 0)
    dh, share = call(
        second_kernel,
        [
            jax.ShapeDtypeStruct((rows, hidden), F32),
            jax.ShapeDtypeStruct((2 * slots, tokens), F32),
        ],
        [total, z2, z3, x2, d3, sib_a, sib_b, weight, hb, place, chosen, row_weight],
        scratch=[pltpu.VMEM((2, rows, width), BF16)],
        flops=half_flops,
    )
    share = share + swap(share, 0, 0, 1) + swap(share, 0, 0, 2) + swap(share, 0, 0, 3)
    pieces = [share, swap(share, 0, 1, 0), swap(share, 1, 0, 0), swap(share, 1, 1, 0)]
    grad_gate, grad_up = call(
        grads_kernel,
        [jax.ShapeDtypeStruct((rows, hidden), BF16)] * 2,
        [dh, gate, up],
    )
    (logit_grad,) = call(
        logits_kernel,
        [jax.ShapeDtypeStruct((2, tokens), F32)],
        [*pieces, logits_t],
        scratch=[pltpu.VMEM((2 * slots, tokens), F32)],
    )
    return grad_gate, grad_up, logit_grad.T


def body(out_grad, router_logits, slot_of, gate_pre, up_pre, down_weight):
    slots = lax.axis_size("expert")
    total_rows = gate_pre.shape[0]
    capacity = total_rows // slots
    weight = down_weight[0]
    first = jax.nn.sigmoid(router_logits[:, 0] - router_logits[:, 1])
    probs = jnp.stack([first, 1.0 - first], axis=1)
    probs_b = probs.astype(jnp.bfloat16)
    flat_slot = slot_of.reshape(-1)
    onehot = (flat_slot[:, None] == jnp.arange(slots, dtype=jnp.int32)[None, :]).astype(jnp.int32)
    earlier = (jnp.cumsum(onehot, axis=0) - onehot) * onehot
    position = jnp.sum(earlier, axis=1)
    dest = flat_slot * capacity + position
    placing = dest[:, None] == jnp.arange(total_rows, dtype=jnp.int32)[None, :]
    place_b = placing.astype(jnp.bfloat16)
    place_f = placing.astype(jnp.float32)
    rows_dy = jnp.repeat(out_grad, 2, axis=0)
    send_rows = lax.dot_general(
        place_b, rows_dy, (((0,), (0,)), ((), ())), preferred_element_type=jnp.float32
    ).astype(jnp.bfloat16)
    send_weight = jnp.dot(probs_b.reshape(-1).astype(jnp.float32), place_f).astype(jnp.bfloat16)
    received, row_weight = (
        lax.all_to_all(send_rows, "expert", split_axis=0, concat_axis=0, tiled=True),
        lax.all_to_all(send_weight, "expert", split_axis=0, concat_axis=0, tiled=True),
    )
    z_local = lax.dot_general(
        lax.all_gather(received, "etp", axis=1, tiled=True),
        weight,
        (((1,), (1,)), ((), ())),
        preferred_element_type=jnp.float32,
    )
    g = gate_pre.astype(jnp.float32)
    u = up_pre.astype(jnp.float32)
    sig = jax.nn.sigmoid(g)
    act = g * sig
    hb = (act * u).astype(jnp.bfloat16)
    dh = row_weight.astype(jnp.float32)[:, None] * z_local
    grad_up = (dh * act).astype(jnp.bfloat16)
    grad_gate = (dh * u * sig * (1.0 + g * (1.0 - sig))).astype(jnp.bfloat16)
    partial_dp = jnp.sum(hb.astype(jnp.float32) * z_local, axis=1)
    row_dp = lax.psum(partial_dp, "etp")
    returned = lax.all_to_all(row_dp, "expert", split_axis=0, concat_axis=0, tiled=True)
    picked = jnp.dot(place_f, returned).reshape(probs.shape)
    mean_term = jnp.sum(probs * picked, axis=1, keepdims=True)
    logit_grad = probs * (picked - mean_term)
    return (grad_gate, grad_up, logit_grad)


def solution(mesh):
    small = mesh.shape["expert"] == 4 and mesh.shape["etp"] == 4
    return jax.shard_map(
        small_body if small else body,
        mesh=mesh,
        in_specs=(
            P(("parts", "expert"), "etp"),
            P(("parts", "expert"), None),
            P(("parts", "expert"), None),
            P(("parts", "expert"), "etp"),
            P(("parts", "expert"), "etp"),
            P("expert", "etp", None),
        ),
        out_specs=(
            P(("parts", "expert"), "etp"),
            P(("parts", "expert"), "etp"),
            P(("parts", "expert"), None),
        ),
        check_vma=False,
    )
```

```python
import jax
import jax.numpy as jnp
from jax import lax
from jax.experimental import pallas as pl
from jax.experimental.pallas import tpu as pltpu
from jax.sharding import PartitionSpec as P

BF16 = jnp.bfloat16
F32 = jnp.float32
NT = (((1,), (1,)), ((), ()))
META = 16


VMEM = pl.BlockSpec(memory_space=pltpu.VMEM)
HBM = pl.BlockSpec(memory_space=pltpu.HBM)


def call(kernel, outs, args, scratch=(), flops=0, limit=16, hbm=0):
    args = [pltpu.with_memory_space_constraint(a, pltpu.HBM) for a in args[:hbm]] + list(args[hbm:])
    out_bytes = sum(o.size * o.dtype.itemsize for o in outs)
    in_bytes = sum(a.size * a.dtype.itemsize for a in args)
    return pl.pallas_call(
        kernel,
        out_shape=tuple(outs),
        in_specs=[HBM] * hbm + [VMEM] * (len(args) - hbm),
        out_specs=tuple([VMEM] * len(outs)),
        scratch_shapes=list(scratch),
        compiler_params=pltpu.CompilerParams(vmem_limit_bytes=limit * 2**20),
        cost_estimate=pl.CostEstimate(
            flops=flops, bytes_accessed=out_bytes + in_bytes, transcendentals=0
        ),
    )(*args)


def pack_kernel(rows_hbm, logits_hbm, slots_hbm, out_ref, logits_ref, slots_ref, sems):
    tokens, width = rows_hbm.shape
    copies = [
        pltpu.make_async_copy(logits_hbm, logits_ref, sems.at[0]),
        pltpu.make_async_copy(slots_hbm, slots_ref, sems.at[1]),
        pltpu.make_async_copy(rows_hbm, out_ref.at[pl.ds(0, tokens)], sems.at[2]),
    ]
    for copy in copies:
        copy.start()
    copies[0].wait()
    copies[1].wait()
    first = jax.nn.sigmoid(logits_ref[0:1, :] - logits_ref[1:2, :])
    facts = jnp.concatenate(
        [slots_ref[...].astype(F32), first, 1.0 - first, jnp.zeros((META - 4, tokens), F32)],
        axis=0,
    )
    out_ref[tokens:, :] = jnp.concatenate(
        [facts, jnp.zeros((META, width - tokens), F32)], axis=1
    ).astype(BF16)
    copies[2].wait()


def load_kernel(
    weight_hbm, gate_hbm, up_hbm,
    weight_ref, gate_ref, up_ref, hb_ref,
    sems,
):
    copies = [
        pltpu.make_async_copy(gate_hbm, gate_ref, sems.at[0]),
        pltpu.make_async_copy(up_hbm, up_ref, sems.at[1]),
        pltpu.make_async_copy(weight_hbm, weight_ref, sems.at[2]),
    ]
    for copy in copies:
        copy.start()
    copies[0].wait()
    copies[1].wait()
    g = gate_ref[...].astype(F32)
    hb_ref[...] = (g * jax.nn.sigmoid(g) * up_ref[...].astype(F32)).astype(BF16)
    copies[2].wait()


def bundle_kernel(a_ref, b_ref, c_ref, order_ref, out_ref):
    tokens = a_ref.shape[0]
    out_ref[:tokens, :] = a_ref[...]
    out_ref[tokens : 2 * tokens, :] = b_ref[...]
    out_ref[2 * tokens :, :] = c_ref[...]


def place_rows(target, index, blocks, mine, tokens):
    for other, block in enumerate(blocks):
        start = pl.multiple_of((mine ^ other) * tokens, tokens)
        target[index, pl.ds(start, tokens), :] = block


def first_kernel(
    z2_ref, z1_ref, d1_ref, own_ref, x_ref, sib_ref, weight_ref,
    total_ref, place_ref, chosen_ref, row_weight_ref,
    rows_s, facts_s,
):
    mine, deep = lax.axis_index("expert"), lax.axis_index("etp")
    tokens, width = z1_ref.shape
    long = tokens + META
    groups = total_ref.shape[0] // tokens
    sib_d1 = long + tokens
    sib_z1 = sib_d1 + tokens
    sib_x = sib_z1 + tokens
    sib_facts = sib_x + tokens
    place_rows(
        rows_s, 0,
        (own_ref[:tokens, :], sib_ref[:tokens, :], x_ref[:tokens, :], sib_ref[sib_x : sib_x + tokens, :]),
        mine, tokens,
    )
    place_rows(
        rows_s, 1,
        (z1_ref[...], sib_ref[sib_z1 : sib_z1 + tokens, :], d1_ref[...], sib_ref[sib_d1 : sib_d1 + tokens, :]),
        mine, tokens,
    )
    for other, (ref, start) in enumerate(
        ((own_ref, tokens), (sib_ref, tokens), (x_ref, tokens), (sib_ref, sib_facts))
    ):
        facts_s[mine ^ other] = ref[start : start + META, :tokens].astype(F32)
    total = None
    for index in range(2):
        start = pl.multiple_of((deep ^ index) * width, 128)
        part = lax.dot_general(
            rows_s[index], weight_ref[:, pl.ds(start, width)], NT, preferred_element_type=F32
        )
        total = part if total is None else total + part
    total_ref[...] = total
    slot = mine.astype(F32)
    row = lax.broadcasted_iota(jnp.int32, (tokens, tokens), 0)
    lane = lax.broadcasted_iota(jnp.int32, (tokens, tokens), 1)
    before = (row < lane).astype(BF16)
    row_f = row.astype(F32)
    firsts = [(facts_s[j, 0:1, :] == slot).astype(F32) for j in range(groups)]
    seconds = [(facts_s[j, 1:2, :] == slot).astype(F32) for j in range(groups)]
    chosen = jnp.concatenate(firsts + seconds, axis=0)
    chosen_ref[...] = chosen
    match = chosen[:groups] + chosen[groups:]
    position = jnp.dot(
        jnp.concatenate([match, match], axis=0).astype(BF16), before, preferred_element_type=F32
    )
    for j in range(groups):
        hit = (position[j : j + 1] == row_f) & (match[j : j + 1] > 0.5)
        place = hit.astype(F32)
        weight = firsts[j] * facts_s[j, 2:3, :] + seconds[j] * facts_s[j, 3:4, :]
        place_ref[j] = place
        row_weight_ref[j * tokens : (j + 1) * tokens, :] = jnp.sum(
            place * weight, axis=1, keepdims=True
        )


def second_kernel(
    total_ref, z2_ref, z3_ref, x2_ref, d3_ref, sib_a_ref, sib_b_ref, weight_ref,
    hb_ref, place_ref, chosen_ref, row_weight_ref,
    dh_ref, share_ref,
    rows_s,
):
    mine, deep = lax.axis_index("expert"), lax.axis_index("etp")
    tokens, width = z2_ref.shape
    groups = total_ref.shape[0] // tokens
    first = tokens + META
    place_rows(
        rows_s, 0,
        (z2_ref[...], sib_a_ref[first : first + tokens, :], x2_ref[...], sib_b_ref[tokens : 2 * tokens, :]),
        mine, tokens,
    )
    place_rows(
        rows_s, 1,
        (z3_ref[...], sib_b_ref[:tokens, :], d3_ref[...], sib_b_ref[2 * tokens :, :]),
        mine, tokens,
    )
    total = total_ref[...]
    for index in range(2):
        start = pl.multiple_of((deep ^ (2 + index)) * width, 128)
        total = total + lax.dot_general(
            rows_s[index], weight_ref[:, pl.ds(start, width)], NT, preferred_element_type=F32
        )
    sums = []
    for j in range(groups):
        part = slice(j * tokens, (j + 1) * tokens)
        place = place_ref[j]
        place_b = place.astype(BF16)
        high = total[part].astype(BF16)
        low = (total[part] - high.astype(F32)).astype(BF16)
        z = jnp.dot(place_b, high, preferred_element_type=F32) + jnp.dot(
            place_b, low, preferred_element_type=F32
        )
        dh_ref[part, :] = row_weight_ref[part, :] * z
        dp = jnp.sum(hb_ref[part, :].astype(F32) * z, axis=1, keepdims=True)
        sums.append(jnp.sum(place * dp, axis=0, keepdims=True))
    sums = jnp.concatenate(sums, axis=0)
    share_ref[...] = chosen_ref[...] * jnp.concatenate([sums, sums], axis=0)


def grads_kernel(dh_ref, gate_ref, up_ref, grad_gate_ref, grad_up_ref):
    g = gate_ref[...].astype(F32)
    u = up_ref[...].astype(F32)
    dh = dh_ref[...]
    sig = jax.nn.sigmoid(g)
    grad_up_ref[...] = (dh * (g * sig)).astype(BF16)
    grad_gate_ref[...] = (dh * u * sig * (1.0 + g * (1.0 - sig))).astype(BF16)


def logits_kernel(a_ref, b_ref, c_ref, d_ref, logits_ref, out_ref, sum_s):
    mine = lax.axis_index("expert")
    groups = a_ref.shape[0] // 2
    sum_s[...] = (a_ref[...] + b_ref[...]) + (c_ref[...] + d_ref[...])
    picked_0 = sum_s[pl.ds(mine, 1), :]
    picked_1 = sum_s[pl.ds(mine + groups, 1), :]
    first = jax.nn.sigmoid(logits_ref[0:1, :] - logits_ref[1:2, :])
    second = 1.0 - first
    mean = first * picked_0 + second * picked_1
    out_ref[...] = jnp.concatenate([first * (picked_0 - mean), second * (picked_1 - mean)], axis=0)


def small_body(out_grad, router_logits, slot_of, gate_pre, up_pre, down_weight):
    tokens, width = out_grad.shape
    rows, hidden = gate_pre.shape
    weight = down_weight[0]
    slots, deep = lax.axis_size("expert"), lax.axis_size("etp")

    def swap(value, dx, dc, dz):
        mask = (dx * 2 + dc) * deep + dz
        return lax.ppermute(
            value, ("expert", "etp"), [(i, i ^ mask) for i in range(slots * deep)]
        )

    logits_t, slots_t = router_logits.T, slot_of.T
    z2 = swap(out_grad, 0, 0, 2)
    z1 = swap(out_grad, 0, 0, 1)
    (own,) = call(
        pack_kernel,
        [jax.ShapeDtypeStruct((tokens + META, width), BF16)],
        [out_grad, logits_t, slots_t],
        scratch=[
            pltpu.VMEM((2, tokens), F32),
            pltpu.VMEM((2, tokens), jnp.int32),
            pltpu.SemaphoreType.DMA((3,)),
        ],
        hbm=3,
    )
    xo = swap(own, 1, 0, 0)
    d1 = swap(out_grad, 1, 0, 1)
    weight, gate, up, hb = call(
        load_kernel,
        [
            jax.ShapeDtypeStruct(weight.shape, BF16),
            jax.ShapeDtypeStruct((rows, hidden), BF16),
            jax.ShapeDtypeStruct((rows, hidden), BF16),
            jax.ShapeDtypeStruct((rows, hidden), BF16),
        ],
        [weight, gate_pre, up_pre],
        scratch=[pltpu.SemaphoreType.DMA((3,))],
        hbm=3,
    )
    z3 = swap(z2, 0, 0, 1)
    x2 = swap(z2, 1, 0, 0)
    d3 = swap(z2, 1, 0, 1)
    sib_a = swap(jnp.concatenate([own, z2, d1, z1, xo], axis=0), 0, 1, 0)
    half_flops = 2 * rows * hidden * width * 2
    total, place, chosen, row_weight = call(
        first_kernel,
        [
            jax.ShapeDtypeStruct((rows, hidden), F32),
            jax.ShapeDtypeStruct((slots, tokens, tokens), F32),
            jax.ShapeDtypeStruct((2 * slots, tokens), F32),
            jax.ShapeDtypeStruct((rows, 1), F32),
        ],
        [z2, z1, d1, own, xo, sib_a, weight],
        scratch=[pltpu.VMEM((2, rows, width), BF16), pltpu.VMEM((slots, META, tokens), F32)],
        flops=half_flops,
    )
    (bundle,) = call(
        bundle_kernel,
        [jax.ShapeDtypeStruct((3 * tokens, width), BF16)],
        [z3, x2, d3, hb],
        flops=4 * 10**9,
    )
    sib_b = swap(bundle, 0, 1, 0)
    dh, share = call(
        second_kernel,
        [
            jax.ShapeDtypeStruct((rows, hidden), F32),
            jax.ShapeDtypeStruct((2 * slots, tokens), F32),
        ],
        [total, z2, z3, x2, d3, sib_a, sib_b, weight, hb, place, chosen, row_weight],
        scratch=[pltpu.VMEM((2, rows, width), BF16)],
        flops=half_flops,
    )
    share = share + swap(share, 0, 0, 1) + swap(share, 0, 0, 2) + swap(share, 0, 0, 3)
    pieces = [share, swap(share, 0, 1, 0), swap(share, 1, 0, 0), swap(share, 1, 1, 0)]
    grad_gate, grad_up = call(
        grads_kernel,
        [jax.ShapeDtypeStruct((rows, hidden), BF16)] * 2,
        [dh, gate, up],
    )
    (logit_grad,) = call(
        logits_kernel,
        [jax.ShapeDtypeStruct((2, tokens), F32)],
        [*pieces, logits_t],
        scratch=[pltpu.VMEM((2 * slots, tokens), F32)],
    )
    return grad_gate, grad_up, logit_grad.T


def body(out_grad, router_logits, slot_of, gate_pre, up_pre, down_weight):
    slots = lax.axis_size("expert")
    total_rows = gate_pre.shape[0]
    capacity = total_rows // slots
    weight = down_weight[0]
    first = jax.nn.sigmoid(router_logits[:, 0] - router_logits[:, 1])
    probs = jnp.stack([first, 1.0 - first], axis=1)
    probs_b = probs.astype(jnp.bfloat16)
    flat_slot = slot_of.reshape(-1)
    onehot = (flat_slot[:, None] == jnp.arange(slots, dtype=jnp.int32)[None, :]).astype(jnp.int32)
    earlier = (jnp.cumsum(onehot, axis=0) - onehot) * onehot
    position = jnp.sum(earlier, axis=1)
    dest = flat_slot * capacity + position
    placing = dest[:, None] == jnp.arange(total_rows, dtype=jnp.int32)[None, :]
    place_b = placing.astype(jnp.bfloat16)
    place_f = placing.astype(jnp.float32)
    rows_dy = jnp.repeat(out_grad, 2, axis=0)
    send_rows = lax.dot_general(
        place_b, rows_dy, (((0,), (0,)), ((), ())), preferred_element_type=jnp.float32
    ).astype(jnp.bfloat16)
    send_weight = jnp.dot(probs_b.reshape(-1).astype(jnp.float32), place_f).astype(jnp.bfloat16)
    received, row_weight = (
        lax.all_to_all(send_rows, "expert", split_axis=0, concat_axis=0, tiled=True),
        lax.all_to_all(send_weight, "expert", split_axis=0, concat_axis=0, tiled=True),
    )
    z_local = lax.dot_general(
        lax.all_gather(received, "etp", axis=1, tiled=True),
        weight,
        (((1,), (1,)), ((), ())),
        preferred_element_type=jnp.float32,
    )
    g = gate_pre.astype(jnp.float32)
    u = up_pre.astype(jnp.float32)
    sig = jax.nn.sigmoid(g)
    act = g * sig
    hb = (act * u).astype(jnp.bfloat16)
    dh = row_weight.astype(jnp.float32)[:, None] * z_local
    grad_up = (dh * act).astype(jnp.bfloat16)
    grad_gate = (dh * u * sig * (1.0 + g * (1.0 - sig))).astype(jnp.bfloat16)
    partial_dp = jnp.sum(hb.astype(jnp.float32) * z_local, axis=1)
    row_dp = lax.psum(partial_dp, "etp")
    returned = lax.all_to_all(row_dp, "expert", split_axis=0, concat_axis=0, tiled=True)
    picked = jnp.dot(place_f, returned).reshape(probs.shape)
    mean_term = jnp.sum(probs * picked, axis=1, keepdims=True)
    logit_grad = probs * (picked - mean_term)
    return (grad_gate, grad_up, logit_grad)


def solution(mesh):
    small = mesh.shape["expert"] == 4 and mesh.shape["etp"] == 4
    return jax.shard_map(
        small_body if small else body,
        mesh=mesh,
        in_specs=(
            P(("parts", "expert"), "etp"),
            P(("parts", "expert"), None),
            P(("parts", "expert"), None),
            P(("parts", "expert"), "etp"),
            P(("parts", "expert"), "etp"),
            P("expert", "etp", None),
        ),
        out_specs=(
            P(("parts", "expert"), "etp"),
            P(("parts", "expert"), "etp"),
            P(("parts", "expert"), None),
        ),
        check_vma=False,
    )
```

```python
import jax
import jax.numpy as jnp
from jax import lax
from jax.experimental import pallas as pl
from jax.experimental.pallas import tpu as pltpu
from jax.sharding import PartitionSpec as P

BF16 = jnp.bfloat16
F32 = jnp.float32
NT = (((1,), (1,)), ((), ()))
META = 16


VMEM = pl.BlockSpec(memory_space=pltpu.VMEM)
HBM = pl.BlockSpec(memory_space=pltpu.HBM)


def call(kernel, outs, args, scratch=(), flops=0, limit=16, hbm=0):
    args = [pltpu.with_memory_space_constraint(a, pltpu.HBM) for a in args[:hbm]] + list(args[hbm:])
    out_bytes = sum(o.size * o.dtype.itemsize for o in outs)
    in_bytes = sum(a.size * a.dtype.itemsize for a in args)
    return pl.pallas_call(
        kernel,
        out_shape=tuple(outs),
        in_specs=[HBM] * hbm + [VMEM] * (len(args) - hbm),
        out_specs=tuple([VMEM] * len(outs)),
        scratch_shapes=list(scratch),
        compiler_params=pltpu.CompilerParams(vmem_limit_bytes=limit * 2**20),
        cost_estimate=pl.CostEstimate(
            flops=flops, bytes_accessed=out_bytes + in_bytes, transcendentals=0
        ),
    )(*args)


def pack_kernel(rows_hbm, logits_hbm, slots_hbm, out_ref, logits_ref, slots_ref, sems):
    tokens, width = rows_hbm.shape
    copies = [
        pltpu.make_async_copy(logits_hbm, logits_ref, sems.at[0]),
        pltpu.make_async_copy(slots_hbm, slots_ref, sems.at[1]),
        pltpu.make_async_copy(rows_hbm, out_ref.at[pl.ds(0, tokens)], sems.at[2]),
    ]
    for copy in copies:
        copy.start()
    copies[0].wait()
    copies[1].wait()
    first = jax.nn.sigmoid(logits_ref[0:1, :] - logits_ref[1:2, :])
    facts = jnp.concatenate(
        [slots_ref[...].astype(F32), first, 1.0 - first, jnp.zeros((META - 4, tokens), F32)],
        axis=0,
    )
    out_ref[tokens:, :] = jnp.concatenate(
        [facts, jnp.zeros((META, width - tokens), F32)], axis=1
    ).astype(BF16)
    copies[2].wait()


def load_kernel(
    weight_hbm, gate_hbm, up_hbm,
    weight_ref, gate_ref, up_ref, hb_ref,
    sems,
):
    copies = [
        pltpu.make_async_copy(gate_hbm, gate_ref, sems.at[0]),
        pltpu.make_async_copy(up_hbm, up_ref, sems.at[1]),
        pltpu.make_async_copy(weight_hbm, weight_ref, sems.at[2]),
    ]
    for copy in copies:
        copy.start()
    copies[0].wait()
    copies[1].wait()
    g = gate_ref[...].astype(F32)
    hb_ref[...] = (g * jax.nn.sigmoid(g) * up_ref[...].astype(F32)).astype(BF16)
    copies[2].wait()


def bundle_kernel(a_ref, b_ref, c_ref, order_ref, out_ref):
    tokens = a_ref.shape[0]
    out_ref[:tokens, :] = a_ref[...]
    out_ref[tokens : 2 * tokens, :] = b_ref[...]
    out_ref[2 * tokens :, :] = c_ref[...]


def place_rows(target, index, blocks, mine, tokens):
    for other, block in enumerate(blocks):
        start = pl.multiple_of((mine ^ other) * tokens, tokens)
        target[index, pl.ds(start, tokens), :] = block


def first_kernel(
    d1_ref, z2_ref, z1_ref, own_ref, x_ref, sib_ref, weight_ref, hb_ref,
    total_ref, token_hb_ref, place_ref, chosen_ref, row_weight_ref,
    rows_s, facts_s,
):
    mine, deep = lax.axis_index("expert"), lax.axis_index("etp")
    tokens, width = z1_ref.shape
    long = tokens + META
    groups = total_ref.shape[0] // tokens
    sib_d1 = long + tokens
    sib_z1 = sib_d1 + tokens
    sib_x = sib_z1 + tokens
    sib_facts = sib_x + tokens
    place_rows(
        rows_s, 0,
        (own_ref[:tokens, :], sib_ref[:tokens, :], x_ref[:tokens, :], sib_ref[sib_x : sib_x + tokens, :]),
        mine, tokens,
    )
    place_rows(
        rows_s, 1,
        (z1_ref[...], sib_ref[sib_z1 : sib_z1 + tokens, :], d1_ref[...], sib_ref[sib_d1 : sib_d1 + tokens, :]),
        mine, tokens,
    )
    for other, (ref, start) in enumerate(
        ((own_ref, tokens), (sib_ref, tokens), (x_ref, tokens), (sib_ref, sib_facts))
    ):
        facts_s[mine ^ other] = ref[start : start + META, :tokens].astype(F32)
    total = None
    for index in range(2):
        start = pl.multiple_of((deep ^ index) * width, 128)
        part = lax.dot_general(
            rows_s[index], weight_ref[:, pl.ds(start, width)], NT, preferred_element_type=F32
        )
        total = part if total is None else total + part
    total_ref[...] = total
    slot = mine.astype(F32)
    row = lax.broadcasted_iota(jnp.int32, (tokens, tokens), 0)
    lane = lax.broadcasted_iota(jnp.int32, (tokens, tokens), 1)
    before = (row < lane).astype(BF16)
    row_f = row.astype(F32)
    firsts = [(facts_s[j, 0:1, :] == slot).astype(F32) for j in range(groups)]
    seconds = [(facts_s[j, 1:2, :] == slot).astype(F32) for j in range(groups)]
    chosen = jnp.concatenate(firsts + seconds, axis=0)
    chosen_ref[...] = chosen
    match = chosen[:groups] + chosen[groups:]
    position = jnp.dot(
        jnp.concatenate([match, match], axis=0).astype(BF16), before, preferred_element_type=F32
    )
    for j in range(groups):
        hit = (position[j : j + 1] == row_f) & (match[j : j + 1] > 0.5)
        place = hit.astype(F32)
        weight = firsts[j] * facts_s[j, 2:3, :] + seconds[j] * facts_s[j, 3:4, :]
        place_ref[j] = place
        token_hb_ref[j * tokens : (j + 1) * tokens, :] = lax.dot_general(
            place.astype(BF16),
            hb_ref[j * tokens : (j + 1) * tokens, :],
            (((0,), (0,)), ((), ())),
            preferred_element_type=F32,
        ).astype(BF16)
        row_weight_ref[j * tokens : (j + 1) * tokens, :] = jnp.sum(
            place * weight, axis=1, keepdims=True
        )


def second_kernel(
    total_ref, z2_ref, d3_ref, x2_ref, z3_ref, sib_a_ref, sib_b_ref, weight_ref,
    token_hb_ref, chosen_ref,
    sum_ref, share_ref,
    rows_s,
):
    mine, deep = lax.axis_index("expert"), lax.axis_index("etp")
    tokens, width = z2_ref.shape
    groups = total_ref.shape[0] // tokens
    first = tokens + META
    place_rows(
        rows_s, 0,
        (z2_ref[...], sib_a_ref[first : first + tokens, :], x2_ref[...], sib_b_ref[tokens : 2 * tokens, :]),
        mine, tokens,
    )
    place_rows(
        rows_s, 1,
        (z3_ref[...], sib_b_ref[:tokens, :], d3_ref[...], sib_b_ref[2 * tokens :, :]),
        mine, tokens,
    )
    total = total_ref[...]
    for index in range(2):
        start = pl.multiple_of((deep ^ (2 + index)) * width, 128)
        total = total + lax.dot_general(
            rows_s[index], weight_ref[:, pl.ds(start, width)], NT, preferred_element_type=F32
        )
    sum_ref[...] = total
    same = (
        lax.broadcasted_iota(jnp.int32, (tokens, tokens), 0)
        == lax.broadcasted_iota(jnp.int32, (tokens, tokens), 1)
    ).astype(F32)
    dp = jnp.sum(token_hb_ref[...].astype(F32) * total, axis=1, keepdims=True)
    sums = [
        jnp.sum(same * dp[j * tokens : (j + 1) * tokens], axis=0, keepdims=True) for j in range(groups)
    ]
    sums = jnp.concatenate(sums, axis=0)
    share_ref[...] = chosen_ref[...] * jnp.concatenate([sums, sums], axis=0)


def grads_kernel(total_ref, place_ref, row_weight_ref, gate_ref, up_ref, grad_gate_ref, grad_up_ref):
    groups, tokens, _ = place_ref.shape
    for j in range(groups):
        part = slice(j * tokens, (j + 1) * tokens)
        place_b = place_ref[j].astype(BF16)
        total = total_ref[part, :]
        high = total.astype(BF16)
        low = (total - high.astype(F32)).astype(BF16)
        z = jnp.dot(place_b, high, preferred_element_type=F32) + jnp.dot(
            place_b, low, preferred_element_type=F32
        )
        dh = row_weight_ref[part, :] * z
        g = gate_ref[part, :].astype(F32)
        u = up_ref[part, :].astype(F32)
        sig = jax.nn.sigmoid(g)
        grad_up_ref[part, :] = (dh * (g * sig)).astype(BF16)
        grad_gate_ref[part, :] = (dh * u * sig * (1.0 + g * (1.0 - sig))).astype(BF16)


def logits_kernel(a_ref, b_ref, c_ref, d_ref, logits_ref, out_ref, sum_s):
    mine = lax.axis_index("expert")
    groups = a_ref.shape[0] // 2
    sum_s[...] = (a_ref[...] + b_ref[...]) + (c_ref[...] + d_ref[...])
    picked_0 = sum_s[pl.ds(mine, 1), :]
    picked_1 = sum_s[pl.ds(mine + groups, 1), :]
    first = jax.nn.sigmoid(logits_ref[0:1, :] - logits_ref[1:2, :])
    second = 1.0 - first
    mean = first * picked_0 + second * picked_1
    out_ref[...] = jnp.concatenate([first * (picked_0 - mean), second * (picked_1 - mean)], axis=0)


def small_body(out_grad, router_logits, slot_of, gate_pre, up_pre, down_weight):
    tokens, width = out_grad.shape
    rows, hidden = gate_pre.shape
    weight = down_weight[0]
    slots, deep = lax.axis_size("expert"), lax.axis_size("etp")

    def swap(value, dx, dc, dz):
        mask = (dx * 2 + dc) * deep + dz
        return lax.ppermute(
            value, ("expert", "etp"), [(i, i ^ mask) for i in range(slots * deep)]
        )

    logits_t, slots_t = router_logits.T, slot_of.T
    z2 = swap(out_grad, 0, 0, 2)
    z1 = swap(out_grad, 0, 0, 1)
    (own,) = call(
        pack_kernel,
        [jax.ShapeDtypeStruct((tokens + META, width), BF16)],
        [out_grad, logits_t, slots_t],
        scratch=[
            pltpu.VMEM((2, tokens), F32),
            pltpu.VMEM((2, tokens), jnp.int32),
            pltpu.SemaphoreType.DMA((3,)),
        ],
        hbm=3,
    )
    xo = swap(own, 1, 0, 0)
    d1 = swap(out_grad, 1, 0, 1)
    weight, gate, up, hb = call(
        load_kernel,
        [
            jax.ShapeDtypeStruct(weight.shape, BF16),
            jax.ShapeDtypeStruct((rows, hidden), BF16),
            jax.ShapeDtypeStruct((rows, hidden), BF16),
            jax.ShapeDtypeStruct((rows, hidden), BF16),
        ],
        [weight, gate_pre, up_pre],
        scratch=[pltpu.SemaphoreType.DMA((3,))],
        hbm=3,
    )
    z3 = swap(z2, 0, 0, 1)
    x2 = swap(z2, 1, 0, 0)
    d3 = swap(z2, 1, 0, 1)
    sib_a = swap(jnp.concatenate([own, z2, d1, z1, xo], axis=0), 0, 1, 0)
    half_flops = 2 * rows * hidden * width * 2
    total, token_hb, place, chosen, row_weight = call(
        first_kernel,
        [
            jax.ShapeDtypeStruct((rows, hidden), F32),
            jax.ShapeDtypeStruct((rows, hidden), BF16),
            jax.ShapeDtypeStruct((slots, tokens, tokens), F32),
            jax.ShapeDtypeStruct((2 * slots, tokens), F32),
            jax.ShapeDtypeStruct((rows, 1), F32),
        ],
        [d1, z2, z1, own, xo, sib_a, weight, hb],
        scratch=[pltpu.VMEM((2, rows, width), BF16), pltpu.VMEM((slots, META, tokens), F32)],
        flops=half_flops,
    )
    (bundle,) = call(
        bundle_kernel,
        [jax.ShapeDtypeStruct((3 * tokens, width), BF16)],
        [z3, x2, d3, hb],
        flops=4 * 10**9,
    )
    sib_b = swap(bundle, 0, 1, 0)
    total, share = call(
        second_kernel,
        [
            jax.ShapeDtypeStruct((rows, hidden), F32),
            jax.ShapeDtypeStruct((2 * slots, tokens), F32),
        ],
        [total, z2, d3, x2, z3, sib_a, sib_b, weight, token_hb, chosen],
        scratch=[pltpu.VMEM((2, rows, width), BF16)],
        flops=half_flops,
    )
    share = share + swap(share, 0, 0, 1) + swap(share, 0, 0, 3) + swap(share, 0, 0, 2)
    pieces = [share, swap(share, 1, 1, 0), swap(share, 1, 0, 0), swap(share, 0, 1, 0)]
    grad_gate, grad_up = call(
        grads_kernel,
        [jax.ShapeDtypeStruct((rows, hidden), BF16)] * 2,
        [total, place, row_weight, gate, up],
    )
    (logit_grad,) = call(
        logits_kernel,
        [jax.ShapeDtypeStruct((2, tokens), F32)],
        [*pieces, logits_t],
        scratch=[pltpu.VMEM((2 * slots, tokens), F32)],
    )
    return grad_gate, grad_up, logit_grad.T


def body(out_grad, router_logits, slot_of, gate_pre, up_pre, down_weight):
    slots = lax.axis_size("expert")
    total_rows = gate_pre.shape[0]
    capacity = total_rows // slots
    weight = down_weight[0]
    first = jax.nn.sigmoid(router_logits[:, 0] - router_logits[:, 1])
    probs = jnp.stack([first, 1.0 - first], axis=1)
    probs_b = probs.astype(jnp.bfloat16)
    flat_slot = slot_of.reshape(-1)
    onehot = (flat_slot[:, None] == jnp.arange(slots, dtype=jnp.int32)[None, :]).astype(jnp.int32)
    earlier = (jnp.cumsum(onehot, axis=0) - onehot) * onehot
    position = jnp.sum(earlier, axis=1)
    dest = flat_slot * capacity + position
    placing = dest[:, None] == jnp.arange(total_rows, dtype=jnp.int32)[None, :]
    place_b = placing.astype(jnp.bfloat16)
    place_f = placing.astype(jnp.float32)
    rows_dy = jnp.repeat(out_grad, 2, axis=0)
    send_rows = lax.dot_general(
        place_b, rows_dy, (((0,), (0,)), ((), ())), preferred_element_type=jnp.float32
    ).astype(jnp.bfloat16)
    send_weight = jnp.dot(probs_b.reshape(-1).astype(jnp.float32), place_f).astype(jnp.bfloat16)
    received, row_weight = (
        lax.all_to_all(send_rows, "expert", split_axis=0, concat_axis=0, tiled=True),
        lax.all_to_all(send_weight, "expert", split_axis=0, concat_axis=0, tiled=True),
    )
    z_local = lax.dot_general(
        lax.all_gather(received, "etp", axis=1, tiled=True),
        weight,
        (((1,), (1,)), ((), ())),
        preferred_element_type=jnp.float32,
    )
    g = gate_pre.astype(jnp.float32)
    u = up_pre.astype(jnp.float32)
    sig = jax.nn.sigmoid(g)
    act = g * sig
    hb = (act * u).astype(jnp.bfloat16)
    dh = row_weight.astype(jnp.float32)[:, None] * z_local
    grad_up = (dh * act).astype(jnp.bfloat16)
    grad_gate = (dh * u * sig * (1.0 + g * (1.0 - sig))).astype(jnp.bfloat16)
    partial_dp = jnp.sum(hb.astype(jnp.float32) * z_local, axis=1)
    row_dp = lax.psum(partial_dp, "etp")
    returned = lax.all_to_all(row_dp, "expert", split_axis=0, concat_axis=0, tiled=True)
    picked = jnp.dot(place_f, returned).reshape(probs.shape)
    mean_term = jnp.sum(probs * picked, axis=1, keepdims=True)
    logit_grad = probs * (picked - mean_term)
    return (grad_gate, grad_up, logit_grad)


def solution(mesh):
    small = mesh.shape["expert"] == 4 and mesh.shape["etp"] == 4
    return jax.shard_map(
        small_body if small else body,
        mesh=mesh,
        in_specs=(
            P(("parts", "expert"), "etp"),
            P(("parts", "expert"), None),
            P(("parts", "expert"), None),
            P(("parts", "expert"), "etp"),
            P(("parts", "expert"), "etp"),
            P("expert", "etp", None),
        ),
        out_specs=(
            P(("parts", "expert"), "etp"),
            P(("parts", "expert"), "etp"),
            P(("parts", "expert"), None),
        ),
        check_vma=False,
    )
```

```python
import jax
import jax.numpy as jnp
from jax import lax
from jax.experimental import pallas as pl
from jax.experimental.pallas import tpu as pltpu
from jax.sharding import PartitionSpec as P

BF16 = jnp.bfloat16
F32 = jnp.float32
NT = (((1,), (1,)), ((), ()))
META = 16


VMEM = pl.BlockSpec(memory_space=pltpu.VMEM)
HBM = pl.BlockSpec(memory_space=pltpu.HBM)


def call(kernel, outs, args, scratch=(), flops=0, limit=16, hbm=0):
    args = [pltpu.with_memory_space_constraint(a, pltpu.HBM) for a in args[:hbm]] + list(args[hbm:])
    out_bytes = sum(o.size * o.dtype.itemsize for o in outs)
    in_bytes = sum(a.size * a.dtype.itemsize for a in args)
    return pl.pallas_call(
        kernel,
        out_shape=tuple(outs),
        in_specs=[HBM] * hbm + [VMEM] * (len(args) - hbm),
        out_specs=tuple([VMEM] * len(outs)),
        scratch_shapes=list(scratch),
        compiler_params=pltpu.CompilerParams(vmem_limit_bytes=limit * 2**20),
        cost_estimate=pl.CostEstimate(
            flops=flops, bytes_accessed=out_bytes + in_bytes, transcendentals=0
        ),
    )(*args)


def pack_kernel(rows_hbm, logits_hbm, slots_hbm, out_ref, logits_ref, slots_ref, sems):
    tokens, width = rows_hbm.shape
    copies = [
        pltpu.make_async_copy(logits_hbm, logits_ref, sems.at[0]),
        pltpu.make_async_copy(slots_hbm, slots_ref, sems.at[1]),
        pltpu.make_async_copy(rows_hbm, out_ref.at[pl.ds(0, tokens)], sems.at[2]),
    ]
    for copy in copies:
        copy.start()
    copies[0].wait()
    copies[1].wait()
    first = jax.nn.sigmoid(logits_ref[0:1, :] - logits_ref[1:2, :])
    facts = jnp.concatenate(
        [slots_ref[...].astype(F32), first, 1.0 - first, jnp.zeros((META - 4, tokens), F32)],
        axis=0,
    )
    out_ref[tokens:, :] = jnp.concatenate(
        [facts, jnp.zeros((META, width - tokens), F32)], axis=1
    ).astype(BF16)
    copies[2].wait()


def half_of(weight_hbm, half):
    width = weight_hbm.shape[1] // 2
    return weight_hbm.at[:, pl.ds(pl.multiple_of(half * width, 128), width)]


def load_kernel(
    weight_hbm, gate_hbm, up_hbm,
    weight_ref, gate_ref, up_ref, hb_ref,
    sems,
):
    copies = [
        pltpu.make_async_copy(gate_hbm, gate_ref, sems.at[0]),
        pltpu.make_async_copy(up_hbm, up_ref, sems.at[1]),
        pltpu.make_async_copy(half_of(weight_hbm, lax.axis_index("etp") // 2), weight_ref, sems.at[2]),
    ]
    for copy in copies:
        copy.start()
    copies[0].wait()
    copies[1].wait()
    g = gate_ref[...].astype(F32)
    hb_ref[...] = (g * jax.nn.sigmoid(g) * up_ref[...].astype(F32)).astype(BF16)
    copies[2].wait()


def other_kernel(weight_hbm, order_ref, weight_ref, sem):
    copy = pltpu.make_async_copy(half_of(weight_hbm, (lax.axis_index("etp") // 2) ^ 1), weight_ref, sem)
    copy.start()
    copy.wait()


def bundle_kernel(a_ref, b_ref, c_ref, order_ref, load_order_ref, out_ref):
    tokens = a_ref.shape[0]
    out_ref[:tokens, :] = a_ref[...]
    out_ref[tokens : 2 * tokens, :] = b_ref[...]
    out_ref[2 * tokens :, :] = c_ref[...]


def place_rows(target, index, blocks, mine, tokens):
    for other, block in enumerate(blocks):
        start = pl.multiple_of((mine ^ other) * tokens, tokens)
        target[index, pl.ds(start, tokens), :] = block


def first_kernel(
    d1_ref, z2_ref, z1_ref, own_ref, x_ref, sib_ref, weight_ref, hb_ref,
    total_ref, token_hb_ref, place_ref, chosen_ref, row_weight_ref,
    rows_s, facts_s,
):
    mine, deep = lax.axis_index("expert"), lax.axis_index("etp")
    tokens, width = z1_ref.shape
    long = tokens + META
    groups = total_ref.shape[0] // tokens
    sib_d1 = long + tokens
    sib_z1 = sib_d1 + tokens
    sib_x = sib_z1 + tokens
    sib_facts = sib_x + tokens
    place_rows(
        rows_s, 0,
        (own_ref[:tokens, :], sib_ref[:tokens, :], x_ref[:tokens, :], sib_ref[sib_x : sib_x + tokens, :]),
        mine, tokens,
    )
    place_rows(
        rows_s, 1,
        (z1_ref[...], sib_ref[sib_z1 : sib_z1 + tokens, :], d1_ref[...], sib_ref[sib_d1 : sib_d1 + tokens, :]),
        mine, tokens,
    )
    for other, (ref, start) in enumerate(
        ((own_ref, tokens), (sib_ref, tokens), (x_ref, tokens), (sib_ref, sib_facts))
    ):
        facts_s[mine ^ other] = ref[start : start + META, :tokens].astype(F32)
    total = None
    for index in range(2):
        start = pl.multiple_of(((deep ^ index) % 2) * width, 128)
        part = lax.dot_general(
            rows_s[index], weight_ref[:, pl.ds(start, width)], NT, preferred_element_type=F32
        )
        total = part if total is None else total + part
    total_ref[...] = total
    slot = mine.astype(F32)
    row = lax.broadcasted_iota(jnp.int32, (tokens, tokens), 0)
    lane = lax.broadcasted_iota(jnp.int32, (tokens, tokens), 1)
    before = (row < lane).astype(BF16)
    row_f = row.astype(F32)
    firsts = [(facts_s[j, 0:1, :] == slot).astype(F32) for j in range(groups)]
    seconds = [(facts_s[j, 1:2, :] == slot).astype(F32) for j in range(groups)]
    chosen = jnp.concatenate(firsts + seconds, axis=0)
    chosen_ref[...] = chosen
    match = chosen[:groups] + chosen[groups:]
    position = jnp.dot(
        jnp.concatenate([match, match], axis=0).astype(BF16), before, preferred_element_type=F32
    )
    for j in range(groups):
        hit = (position[j : j + 1] == row_f) & (match[j : j + 1] > 0.5)
        place = hit.astype(F32)
        weight = firsts[j] * facts_s[j, 2:3, :] + seconds[j] * facts_s[j, 3:4, :]
        place_ref[j] = place
        token_hb_ref[j * tokens : (j + 1) * tokens, :] = lax.dot_general(
            place.astype(BF16),
            hb_ref[j * tokens : (j + 1) * tokens, :],
            (((0,), (0,)), ((), ())),
            preferred_element_type=F32,
        ).astype(BF16)
        row_weight_ref[j * tokens : (j + 1) * tokens, :] = jnp.sum(
            place * weight, axis=1, keepdims=True
        )


def second_kernel(
    total_ref, z2_ref, d3_ref, x2_ref, z3_ref, sib_a_ref, sib_b_ref, weight_ref,
    token_hb_ref, chosen_ref,
    sum_ref, share_ref,
    rows_s,
):
    mine, deep = lax.axis_index("expert"), lax.axis_index("etp")
    tokens, width = z2_ref.shape
    groups = total_ref.shape[0] // tokens
    first = tokens + META
    place_rows(
        rows_s, 0,
        (z2_ref[...], sib_a_ref[first : first + tokens, :], x2_ref[...], sib_b_ref[tokens : 2 * tokens, :]),
        mine, tokens,
    )
    place_rows(
        rows_s, 1,
        (z3_ref[...], sib_b_ref[:tokens, :], d3_ref[...], sib_b_ref[2 * tokens :, :]),
        mine, tokens,
    )
    total = total_ref[...]
    for index in range(2):
        start = pl.multiple_of(((deep ^ index) % 2) * width, 128)
        total = total + lax.dot_general(
            rows_s[index], weight_ref[:, pl.ds(start, width)], NT, preferred_element_type=F32
        )
    sum_ref[...] = total
    same = (
        lax.broadcasted_iota(jnp.int32, (tokens, tokens), 0)
        == lax.broadcasted_iota(jnp.int32, (tokens, tokens), 1)
    ).astype(F32)
    dp = jnp.sum(token_hb_ref[...].astype(F32) * total, axis=1, keepdims=True)
    sums = [
        jnp.sum(same * dp[j * tokens : (j + 1) * tokens], axis=0, keepdims=True) for j in range(groups)
    ]
    sums = jnp.concatenate(sums, axis=0)
    share_ref[...] = chosen_ref[...] * jnp.concatenate([sums, sums], axis=0)


def grads_kernel(total_ref, place_ref, row_weight_ref, gate_ref, up_ref, grad_gate_ref, grad_up_ref):
    groups, tokens, _ = place_ref.shape
    for j in range(groups):
        part = slice(j * tokens, (j + 1) * tokens)
        place_b = place_ref[j].astype(BF16)
        total = total_ref[part, :]
        high = total.astype(BF16)
        low = (total - high.astype(F32)).astype(BF16)
        z = jnp.dot(place_b, high, preferred_element_type=F32) + jnp.dot(
            place_b, low, preferred_element_type=F32
        )
        dh = row_weight_ref[part, :] * z
        g = gate_ref[part, :].astype(F32)
        u = up_ref[part, :].astype(F32)
        sig = jax.nn.sigmoid(g)
        grad_up_ref[part, :] = (dh * (g * sig)).astype(BF16)
        grad_gate_ref[part, :] = (dh * u * sig * (1.0 + g * (1.0 - sig))).astype(BF16)


def logits_kernel(a_ref, b_ref, c_ref, d_ref, logits_ref, out_ref, sum_s):
    mine = lax.axis_index("expert")
    groups = a_ref.shape[0] // 2
    sum_s[...] = (a_ref[...] + b_ref[...]) + (c_ref[...] + d_ref[...])
    picked_0 = sum_s[pl.ds(mine, 1), :]
    picked_1 = sum_s[pl.ds(mine + groups, 1), :]
    first = jax.nn.sigmoid(logits_ref[0:1, :] - logits_ref[1:2, :])
    second = 1.0 - first
    mean = first * picked_0 + second * picked_1
    out_ref[...] = jnp.concatenate([first * (picked_0 - mean), second * (picked_1 - mean)], axis=0)


def small_body(out_grad, router_logits, slot_of, gate_pre, up_pre, down_weight):
    tokens, width = out_grad.shape
    rows, hidden = gate_pre.shape
    weight = down_weight[0]
    slots, deep = lax.axis_size("expert"), lax.axis_size("etp")

    def swap(value, dx, dc, dz):
        mask = (dx * 2 + dc) * deep + dz
        return lax.ppermute(
            value, ("expert", "etp"), [(i, i ^ mask) for i in range(slots * deep)]
        )

    logits_t, slots_t = router_logits.T, slot_of.T
    z2 = swap(out_grad, 0, 0, 2)
    (own,) = call(
        pack_kernel,
        [jax.ShapeDtypeStruct((tokens + META, width), BF16)],
        [out_grad, logits_t, slots_t],
        scratch=[
            pltpu.VMEM((2, tokens), F32),
            pltpu.VMEM((2, tokens), jnp.int32),
            pltpu.SemaphoreType.DMA((3,)),
        ],
        hbm=3,
    )
    rows_here = own[:tokens]
    z1 = swap(rows_here, 0, 0, 1)
    xo = swap(own, 1, 0, 0)
    d1 = swap(rows_here, 1, 0, 1)
    weight_a, gate, up, hb = call(
        load_kernel,
        [
            jax.ShapeDtypeStruct((hidden, 2 * width), BF16),
            jax.ShapeDtypeStruct((rows, hidden), BF16),
            jax.ShapeDtypeStruct((rows, hidden), BF16),
            jax.ShapeDtypeStruct((rows, hidden), BF16),
        ],
        [weight, gate_pre, up_pre],
        scratch=[pltpu.SemaphoreType.DMA((3,))],
        hbm=3,
    )
    z3 = swap(z2, 0, 0, 1)
    x2 = swap(z2, 1, 0, 0)
    d3 = swap(z2, 1, 0, 1)
    sib_a = swap(jnp.concatenate([own, z2, d1, z1, xo], axis=0), 0, 1, 0)
    half_flops = 2 * rows * hidden * width * 2
    total, token_hb, place, chosen, row_weight = call(
        first_kernel,
        [
            jax.ShapeDtypeStruct((rows, hidden), F32),
            jax.ShapeDtypeStruct((rows, hidden), BF16),
            jax.ShapeDtypeStruct((slots, tokens, tokens), F32),
            jax.ShapeDtypeStruct((2 * slots, tokens), F32),
            jax.ShapeDtypeStruct((rows, 1), F32),
        ],
        [d1, z2, z1, own, xo, sib_a, weight_a, hb],
        scratch=[pltpu.VMEM((2, rows, width), BF16), pltpu.VMEM((slots, META, tokens), F32)],
        flops=half_flops,
    )
    (weight_b,) = call(
        other_kernel,
        [jax.ShapeDtypeStruct((hidden, 2 * width), BF16)],
        [weight, xo],
        scratch=[pltpu.SemaphoreType.DMA],
        hbm=1,
    )
    (bundle,) = call(
        bundle_kernel,
        [jax.ShapeDtypeStruct((3 * tokens, width), BF16)],
        [z3, x2, d3, weight_b, hb],
        flops=4 * 10**9,
    )
    sib_b = swap(bundle, 0, 1, 0)
    total, share = call(
        second_kernel,
        [
            jax.ShapeDtypeStruct((rows, hidden), F32),
            jax.ShapeDtypeStruct((2 * slots, tokens), F32),
        ],
        [total, z2, d3, x2, z3, sib_a, sib_b, weight_b, token_hb, chosen],
        scratch=[pltpu.VMEM((2, rows, width), BF16)],
        flops=half_flops,
    )
    share = share + swap(share, 0, 0, 1) + swap(share, 0, 0, 3) + swap(share, 0, 0, 2)
    pieces = [share, swap(share, 1, 1, 0), swap(share, 1, 0, 0), swap(share, 0, 1, 0)]
    grad_gate, grad_up = call(
        grads_kernel,
        [jax.ShapeDtypeStruct((rows, hidden), BF16)] * 2,
        [total, place, row_weight, gate, up],
    )
    (logit_grad,) = call(
        logits_kernel,
        [jax.ShapeDtypeStruct((2, tokens), F32)],
        [*pieces, logits_t],
        scratch=[pltpu.VMEM((2 * slots, tokens), F32)],
    )
    return grad_gate, grad_up, logit_grad.T


def body(out_grad, router_logits, slot_of, gate_pre, up_pre, down_weight):
    slots = lax.axis_size("expert")
    total_rows = gate_pre.shape[0]
    capacity = total_rows // slots
    weight = down_weight[0]
    first = jax.nn.sigmoid(router_logits[:, 0] - router_logits[:, 1])
    probs = jnp.stack([first, 1.0 - first], axis=1)
    probs_b = probs.astype(jnp.bfloat16)
    flat_slot = slot_of.reshape(-1)
    onehot = (flat_slot[:, None] == jnp.arange(slots, dtype=jnp.int32)[None, :]).astype(jnp.int32)
    earlier = (jnp.cumsum(onehot, axis=0) - onehot) * onehot
    position = jnp.sum(earlier, axis=1)
    dest = flat_slot * capacity + position
    placing = dest[:, None] == jnp.arange(total_rows, dtype=jnp.int32)[None, :]
    place_b = placing.astype(jnp.bfloat16)
    place_f = placing.astype(jnp.float32)
    rows_dy = jnp.repeat(out_grad, 2, axis=0)
    send_rows = lax.dot_general(
        place_b, rows_dy, (((0,), (0,)), ((), ())), preferred_element_type=jnp.float32
    ).astype(jnp.bfloat16)
    send_weight = jnp.dot(probs_b.reshape(-1).astype(jnp.float32), place_f).astype(jnp.bfloat16)
    received, row_weight = (
        lax.all_to_all(send_rows, "expert", split_axis=0, concat_axis=0, tiled=True),
        lax.all_to_all(send_weight, "expert", split_axis=0, concat_axis=0, tiled=True),
    )
    z_local = lax.dot_general(
        lax.all_gather(received, "etp", axis=1, tiled=True),
        weight,
        (((1,), (1,)), ((), ())),
        preferred_element_type=jnp.float32,
    )
    g = gate_pre.astype(jnp.float32)
    u = up_pre.astype(jnp.float32)
    sig = jax.nn.sigmoid(g)
    act = g * sig
    hb = (act * u).astype(jnp.bfloat16)
    dh = row_weight.astype(jnp.float32)[:, None] * z_local
    grad_up = (dh * act).astype(jnp.bfloat16)
    grad_gate = (dh * u * sig * (1.0 + g * (1.0 - sig))).astype(jnp.bfloat16)
    partial_dp = jnp.sum(hb.astype(jnp.float32) * z_local, axis=1)
    row_dp = lax.psum(partial_dp, "etp")
    returned = lax.all_to_all(row_dp, "expert", split_axis=0, concat_axis=0, tiled=True)
    picked = jnp.dot(place_f, returned).reshape(probs.shape)
    mean_term = jnp.sum(probs * picked, axis=1, keepdims=True)
    logit_grad = probs * (picked - mean_term)
    return (grad_gate, grad_up, logit_grad)


def solution(mesh):
    small = mesh.shape["expert"] == 4 and mesh.shape["etp"] == 4
    return jax.shard_map(
        small_body if small else body,
        mesh=mesh,
        in_specs=(
            P(("parts", "expert"), "etp"),
            P(("parts", "expert"), None),
            P(("parts", "expert"), None),
            P(("parts", "expert"), "etp"),
            P(("parts", "expert"), "etp"),
            P("expert", "etp", None),
        ),
        out_specs=(
            P(("parts", "expert"), "etp"),
            P(("parts", "expert"), "etp"),
            P(("parts", "expert"), None),
        ),
        check_vma=False,
    )
```

```python
import jax
import jax.numpy as jnp
from jax import lax
from jax.experimental import pallas as pl
from jax.experimental.pallas import tpu as pltpu
from jax.sharding import PartitionSpec as P

BF16 = jnp.bfloat16
F32 = jnp.float32
NT = (((1,), (1,)), ((), ()))
META = 16


VMEM = pl.BlockSpec(memory_space=pltpu.VMEM)
HBM = pl.BlockSpec(memory_space=pltpu.HBM)


def call(kernel, outs, args, scratch=(), flops=0, limit=16, hbm=0):
    args = [pltpu.with_memory_space_constraint(a, pltpu.HBM) for a in args[:hbm]] + list(args[hbm:])
    out_bytes = sum(o.size * o.dtype.itemsize for o in outs)
    in_bytes = sum(a.size * a.dtype.itemsize for a in args)
    return pl.pallas_call(
        kernel,
        out_shape=tuple(outs),
        in_specs=[HBM] * hbm + [VMEM] * (len(args) - hbm),
        out_specs=tuple([VMEM] * len(outs)),
        scratch_shapes=list(scratch),
        compiler_params=pltpu.CompilerParams(vmem_limit_bytes=limit * 2**20),
        cost_estimate=pl.CostEstimate(
            flops=flops, bytes_accessed=out_bytes + in_bytes, transcendentals=0
        ),
    )(*args)


def pack_kernel(rows_hbm, logits_hbm, slots_hbm, out_ref, logits_ref, slots_ref, sems):
    tokens, width = rows_hbm.shape
    copies = [
        pltpu.make_async_copy(logits_hbm, logits_ref, sems.at[0]),
        pltpu.make_async_copy(slots_hbm, slots_ref, sems.at[1]),
        pltpu.make_async_copy(rows_hbm, out_ref.at[pl.ds(0, tokens)], sems.at[2]),
    ]
    for copy in copies:
        copy.start()
    copies[0].wait()
    copies[1].wait()
    first = jax.nn.sigmoid(logits_ref[0:1, :] - logits_ref[1:2, :])
    facts = jnp.concatenate(
        [slots_ref[...].astype(F32), first, 1.0 - first, jnp.zeros((META - 4, tokens), F32)],
        axis=0,
    )
    out_ref[tokens:, :] = jnp.concatenate(
        [facts, jnp.zeros((META, width - tokens), F32)], axis=1
    ).astype(BF16)
    copies[2].wait()


def load_kernel(
    weight_hbm, gate_hbm, up_hbm,
    weight_ref, gate_ref, up_ref, hb_ref,
    sems,
):
    copies = [
        pltpu.make_async_copy(gate_hbm, gate_ref, sems.at[0]),
        pltpu.make_async_copy(up_hbm, up_ref, sems.at[1]),
        pltpu.make_async_copy(weight_hbm, weight_ref, sems.at[2]),
    ]
    for copy in copies:
        copy.start()
    copies[0].wait()
    copies[1].wait()
    g = gate_ref[...].astype(F32)
    hb_ref[...] = (g * jax.nn.sigmoid(g) * up_ref[...].astype(F32)).astype(BF16)
    copies[2].wait()


def bundle_kernel(a_ref, b_ref, c_ref, order_ref, out_ref):
    tokens = a_ref.shape[0]
    out_ref[:tokens, :] = a_ref[...]
    out_ref[tokens : 2 * tokens, :] = b_ref[...]
    out_ref[2 * tokens :, :] = c_ref[...]


def place_rows(target, index, blocks, mine, tokens):
    for other, block in enumerate(blocks):
        start = pl.multiple_of((mine ^ other) * tokens, tokens)
        target[index, pl.ds(start, tokens), :] = block


def first_kernel(
    z2_ref, z1_ref, d1_ref, own_ref, x_ref, sib_ref, weight_ref,
    total_ref, place_ref, chosen_ref, row_weight_ref,
    rows_s, facts_s,
):
    mine, deep = lax.axis_index("expert"), lax.axis_index("etp")
    tokens, width = z1_ref.shape
    long = tokens + META
    groups = total_ref.shape[0] // tokens
    sib_d1 = long + tokens
    sib_z1 = sib_d1 + tokens
    sib_x = sib_z1 + tokens
    sib_facts = sib_x + tokens
    place_rows(
        rows_s, 0,
        (own_ref[:tokens, :], sib_ref[:tokens, :], x_ref[:tokens, :], sib_ref[sib_x : sib_x + tokens, :]),
        mine, tokens,
    )
    place_rows(
        rows_s, 1,
        (z1_ref[...], sib_ref[sib_z1 : sib_z1 + tokens, :], d1_ref[...], sib_ref[sib_d1 : sib_d1 + tokens, :]),
        mine, tokens,
    )
    for other, (ref, start) in enumerate(
        ((own_ref, tokens), (sib_ref, tokens), (x_ref, tokens), (sib_ref, sib_facts))
    ):
        facts_s[mine ^ other] = ref[start : start + META, :tokens].astype(F32)
    total = None
    for index in range(2):
        start = pl.multiple_of((deep ^ index) * width, 128)
        part = lax.dot_general(
            rows_s[index], weight_ref[:, pl.ds(start, width)], NT, preferred_element_type=F32
        )
        total = part if total is None else total + part
    total_ref[...] = total
    slot = mine.astype(F32)
    row = lax.broadcasted_iota(jnp.int32, (tokens, tokens), 0)
    lane = lax.broadcasted_iota(jnp.int32, (tokens, tokens), 1)
    before = (row < lane).astype(BF16)
    row_f = row.astype(F32)
    firsts = [(facts_s[j, 0:1, :] == slot).astype(F32) for j in range(groups)]
    seconds = [(facts_s[j, 1:2, :] == slot).astype(F32) for j in range(groups)]
    chosen = jnp.concatenate(firsts + seconds, axis=0)
    chosen_ref[...] = chosen
    match = chosen[:groups] + chosen[groups:]
    position = jnp.dot(
        jnp.concatenate([match, match], axis=0).astype(BF16), before, preferred_element_type=F32
    )
    for j in range(groups):
        hit = (position[j : j + 1] == row_f) & (match[j : j + 1] > 0.5)
        place = hit.astype(F32)
        weight = firsts[j] * facts_s[j, 2:3, :] + seconds[j] * facts_s[j, 3:4, :]
        place_ref[j] = place
        row_weight_ref[j * tokens : (j + 1) * tokens, :] = jnp.sum(
            place * weight, axis=1, keepdims=True
        )


def second_kernel(
    total_ref, z2_ref, z3_ref, x2_ref, d3_ref, sib_a_ref, sib_b_ref, weight_ref,
    hb_ref, place_ref, chosen_ref, row_weight_ref,
    dh_ref, share_ref,
    rows_s,
):
    mine, deep = lax.axis_index("expert"), lax.axis_index("etp")
    tokens, width = z2_ref.shape
    groups = total_ref.shape[0] // tokens
    first = tokens + META
    place_rows(
        rows_s, 0,
        (z2_ref[...], sib_a_ref[first : first + tokens, :], x2_ref[...], sib_b_ref[tokens : 2 * tokens, :]),
        mine, tokens,
    )
    place_rows(
        rows_s, 1,
        (z3_ref[...], sib_b_ref[:tokens, :], d3_ref[...], sib_b_ref[2 * tokens :, :]),
        mine, tokens,
    )
    total = total_ref[...]
    for index in range(2):
        start = pl.multiple_of((deep ^ (2 + index)) * width, 128)
        total = total + lax.dot_general(
            rows_s[index], weight_ref[:, pl.ds(start, width)], NT, preferred_element_type=F32
        )
    sums = []
    for j in range(groups):
        part = slice(j * tokens, (j + 1) * tokens)
        place = place_ref[j]
        place_b = place.astype(BF16)
        high = total[part].astype(BF16)
        low = (total[part] - high.astype(F32)).astype(BF16)
        z = jnp.dot(place_b, high, preferred_element_type=F32) + jnp.dot(
            place_b, low, preferred_element_type=F32
        )
        dh_ref[part, :] = row_weight_ref[part, :] * z
        dp = jnp.sum(hb_ref[part, :].astype(F32) * z, axis=1, keepdims=True)
        sums.append(jnp.sum(place * dp, axis=0, keepdims=True))
    sums = jnp.concatenate(sums, axis=0)
    share_ref[...] = chosen_ref[...] * jnp.concatenate([sums, sums], axis=0)


def grads_kernel(dh_ref, gate_ref, up_ref, grad_gate_ref, grad_up_ref, zero_ref):
    g = gate_ref[...].astype(F32)
    u = up_ref[...].astype(F32)
    dh = dh_ref[...]
    sig = jax.nn.sigmoid(g)
    grad_up_ref[...] = (dh * (g * sig)).astype(BF16)
    grad_gate_ref[...] = (dh * u * sig * (1.0 + g * (1.0 - sig))).astype(BF16)
    zero_ref[...] = jnp.zeros_like(zero_ref)


def logits_kernel(a_ref, b_ref, c_ref, d_ref, logits_ref, out_ref, sum_s):
    mine = lax.axis_index("expert")
    groups = a_ref.shape[0] // 2
    sum_s[...] = (a_ref[...] + b_ref[...]) + (c_ref[...] + d_ref[...])
    picked_0 = sum_s[pl.ds(mine, 1), :]
    picked_1 = sum_s[pl.ds(mine + groups, 1), :]
    first = jax.nn.sigmoid(logits_ref[0:1, :] - logits_ref[1:2, :])
    second = 1.0 - first
    mean = first * picked_0 + second * picked_1
    out_ref[...] = jnp.concatenate([first * (picked_0 - mean), second * (picked_1 - mean)], axis=0)


def small_body(out_grad, router_logits, slot_of, gate_pre, up_pre, down_weight):
    tokens, width = out_grad.shape
    rows, hidden = gate_pre.shape
    weight = down_weight[0]
    slots, deep = lax.axis_size("expert"), lax.axis_size("etp")

    def swap(value, dx, dc, dz):
        mask = (dx * 2 + dc) * deep + dz
        return lax.ppermute(
            value, ("expert", "etp"), [(i, i ^ mask) for i in range(slots * deep)]
        )

    logits_t, slots_t = router_logits.T, slot_of.T
    z2 = swap(out_grad, 0, 0, 2)
    z1 = swap(out_grad, 0, 0, 1)
    (own,) = call(
        pack_kernel,
        [jax.ShapeDtypeStruct((tokens + META, width), BF16)],
        [out_grad, logits_t, slots_t],
        scratch=[
            pltpu.VMEM((2, tokens), F32),
            pltpu.VMEM((2, tokens), jnp.int32),
            pltpu.SemaphoreType.DMA((3,)),
        ],
        hbm=3,
    )
    xo = swap(own, 1, 0, 0)
    d1 = swap(out_grad, 1, 0, 1)
    weight, gate, up, hb = call(
        load_kernel,
        [
            jax.ShapeDtypeStruct(weight.shape, BF16),
            jax.ShapeDtypeStruct((rows, hidden), BF16),
            jax.ShapeDtypeStruct((rows, hidden), BF16),
            jax.ShapeDtypeStruct((rows, hidden), BF16),
        ],
        [weight, gate_pre, up_pre],
        scratch=[pltpu.SemaphoreType.DMA((3,))],
        hbm=3,
    )
    z3 = swap(z2, 0, 0, 1)
    x2 = swap(z2, 1, 0, 0)
    d3 = swap(z2, 1, 0, 1)
    sib_a = swap(jnp.concatenate([own, z2, d1, z1, xo], axis=0), 0, 1, 0)
    half_flops = 2 * rows * hidden * width * 2
    total, place, chosen, row_weight = call(
        first_kernel,
        [
            jax.ShapeDtypeStruct((rows, hidden), F32),
            jax.ShapeDtypeStruct((slots, tokens, tokens), F32),
            jax.ShapeDtypeStruct((2 * slots, tokens), F32),
            jax.ShapeDtypeStruct((rows, 1), F32),
        ],
        [z2, z1, d1, own, xo, sib_a, weight],
        scratch=[pltpu.VMEM((2, rows, width), BF16), pltpu.VMEM((slots, META, tokens), F32)],
        flops=half_flops,
    )
    (bundle,) = call(
        bundle_kernel,
        [jax.ShapeDtypeStruct((3 * tokens, width), BF16)],
        [z3, x2, d3, hb],
        flops=4 * 10**9,
    )
    sib_b = swap(bundle, 0, 1, 0)
    dh, share = call(
        second_kernel,
        [
            jax.ShapeDtypeStruct((rows, hidden), F32),
            jax.ShapeDtypeStruct((2 * slots, tokens), F32),
        ],
        [total, z2, z3, x2, d3, sib_a, sib_b, weight, hb, place, chosen, row_weight],
        scratch=[pltpu.VMEM((2, rows, width), BF16)],
        flops=half_flops,
    )
    grad_gate, grad_up, zero = call(
        grads_kernel,
        [jax.ShapeDtypeStruct((rows, hidden), BF16)] * 2
        + [jax.ShapeDtypeStruct((2 * slots, tokens), F32)],
        [dh, gate, up],
    )
    share = share + swap(share, 0, 0, 1) + swap(share, 0, 0, 2) + swap(share, 0, 0, 3) + zero
    pieces = [share, swap(share, 0, 1, 0), swap(share, 1, 0, 0), swap(share, 1, 1, 0)]
    (logit_grad,) = call(
        logits_kernel,
        [jax.ShapeDtypeStruct((2, tokens), F32)],
        [*pieces, logits_t],
        scratch=[pltpu.VMEM((2 * slots, tokens), F32)],
    )
    return grad_gate, grad_up, logit_grad.T


def body(out_grad, router_logits, slot_of, gate_pre, up_pre, down_weight):
    slots = lax.axis_size("expert")
    total_rows = gate_pre.shape[0]
    capacity = total_rows // slots
    weight = down_weight[0]
    first = jax.nn.sigmoid(router_logits[:, 0] - router_logits[:, 1])
    probs = jnp.stack([first, 1.0 - first], axis=1)
    probs_b = probs.astype(jnp.bfloat16)
    flat_slot = slot_of.reshape(-1)
    onehot = (flat_slot[:, None] == jnp.arange(slots, dtype=jnp.int32)[None, :]).astype(jnp.int32)
    earlier = (jnp.cumsum(onehot, axis=0) - onehot) * onehot
    position = jnp.sum(earlier, axis=1)
    dest = flat_slot * capacity + position
    placing = dest[:, None] == jnp.arange(total_rows, dtype=jnp.int32)[None, :]
    place_b = placing.astype(jnp.bfloat16)
    place_f = placing.astype(jnp.float32)
    rows_dy = jnp.repeat(out_grad, 2, axis=0)
    send_rows = lax.dot_general(
        place_b, rows_dy, (((0,), (0,)), ((), ())), preferred_element_type=jnp.float32
    ).astype(jnp.bfloat16)
    send_weight = jnp.dot(probs_b.reshape(-1).astype(jnp.float32), place_f).astype(jnp.bfloat16)
    received, row_weight = (
        lax.all_to_all(send_rows, "expert", split_axis=0, concat_axis=0, tiled=True),
        lax.all_to_all(send_weight, "expert", split_axis=0, concat_axis=0, tiled=True),
    )
    z_local = lax.dot_general(
        lax.all_gather(received, "etp", axis=1, tiled=True),
        weight,
        (((1,), (1,)), ((), ())),
        preferred_element_type=jnp.float32,
    )
    g = gate_pre.astype(jnp.float32)
    u = up_pre.astype(jnp.float32)
    sig = jax.nn.sigmoid(g)
    act = g * sig
    hb = (act * u).astype(jnp.bfloat16)
    dh = row_weight.astype(jnp.float32)[:, None] * z_local
    grad_up = (dh * act).astype(jnp.bfloat16)
    grad_gate = (dh * u * sig * (1.0 + g * (1.0 - sig))).astype(jnp.bfloat16)
    partial_dp = jnp.sum(hb.astype(jnp.float32) * z_local, axis=1)
    row_dp = lax.psum(partial_dp, "etp")
    returned = lax.all_to_all(row_dp, "expert", split_axis=0, concat_axis=0, tiled=True)
    picked = jnp.dot(place_f, returned).reshape(probs.shape)
    mean_term = jnp.sum(probs * picked, axis=1, keepdims=True)
    logit_grad = probs * (picked - mean_term)
    return (grad_gate, grad_up, logit_grad)


def solution(mesh):
    small = mesh.shape["expert"] == 4 and mesh.shape["etp"] == 4
    return jax.shard_map(
        small_body if small else body,
        mesh=mesh,
        in_specs=(
            P(("parts", "expert"), "etp"),
            P(("parts", "expert"), None),
            P(("parts", "expert"), None),
            P(("parts", "expert"), "etp"),
            P(("parts", "expert"), "etp"),
            P("expert", "etp", None),
        ),
        out_specs=(
            P(("parts", "expert"), "etp"),
            P(("parts", "expert"), "etp"),
            P(("parts", "expert"), None),
        ),
        check_vma=False,
    )
```
